32 devices in a mesh: prompt: 4 (over z), seq: 8 (over y, x, core).
Axes of the slice: x: 2, y: 2, z: 4, core: 2. Of those that a mesh axis runs over, the one named last changes fastest.
Arguments:
- queries: bfloat16 [4, 8, 2, 32, 128], P('prompt', 'seq'), may hold values from -160 to 160
- prompt_key_cache: bfloat16 [4, 4, 2048, 128], P('prompt', None, 'seq'), may hold values from -5 to 5
- prompt_value_cache: bfloat16 [4, 4, 2048, 128], P('prompt', None, 'seq'), may hold values from -6 to 6
- kept: int32 [4, 4, 8], P('prompt', None, 'seq'), may hold values from 1 to 2, as said below
- sample_keys: bfloat16 [4, 8, 4, 256, 128], P('prompt', 'seq'), may hold values from -6 to 6
- sample_values: bfloat16 [4, 8, 4, 256, 128], P('prompt', 'seq'), may hold values from -6 to 6
- suffix_len: int32 [4, 8], P('prompt', 'seq'), may hold values from 1 to 256, as said below
- decode_keys: bfloat16 [4, 8, 2, 4, 128], P('prompt', 'seq'), may hold values from -6 to 6
- decode_values: bfloat16 [4, 8, 2, 4, 128], P('prompt', 'seq'), may hold values from -6 to 6
- out_weight: bfloat16 [4096, 8192], P('seq', 'prompt'), may hold values from -0.1875 to 0.1875
Outputs:
- attn_out: bfloat16 [64, 8192], P('seq', 'prompt')
The draws below stay inside these ranges and needn't reach their ends.
Inputs may be any that keep to these rules, and one draw needn't show every extreme that they name: `kept`: for every prompt and key-value head some seq index has all 2 slots live. `suffix_len`: in every prompt some sample has 256 generated tokens.
All inputs are finite; a program needn't handle non-finite values.
Results may differ from the reference program's by a relative error of at most 0.0048.
Values may be sent and summed in bfloat16 or wider, within the bound.
No kernel may reach another device: no remote copies, remote signals or barrier semaphores. Data moves between devices by JAX's collectives and lax.ppermute only.
A program may use at most 128 MiB of HBM per device.

```python
import math
import jax
import jax.numpy as jnp
from jax import lax

D = 8192
KEY_VALUE_HEADS = 4
QUERY_GROUP = 8
HEAD_SIZE = 128
BLOCK_TOKENS = 128
DECODE_STEPS = 2
KEPT_SLOTS = 2
SUFFIX_LENGTH = 256
HQ = 32
PROMPT_COUNT = 4
SAMPLE_COUNT = 8
PROMPT_LENGTH = 2048
ROWS = 64
N_SEQ = 8


def joint_draw(key):
    base_offset = jax.random.fold_in(key, 101)
    key_layout = (PROMPT_COUNT, KEY_VALUE_HEADS, N_SEQ * KEPT_SLOTS * BLOCK_TOKENS, HEAD_SIZE)
    query_shape = (PROMPT_COUNT, SAMPLE_COUNT, DECODE_STEPS, HQ, HEAD_SIZE)
    scale_shape = (PROMPT_COUNT, SAMPLE_COUNT, DECODE_STEPS, HQ, 1)
    row_scale = jnp.exp(jax.random.uniform(jax.random.fold_in(base_offset, 5), scale_shape, jnp.float32, math.log(2.5), math.log(15.0)))
    key_cache_store = jnp.clip(jax.random.normal(jax.random.fold_in(base_offset, 1), key_layout, jnp.float32), -5.0, 5.0)
    query_tile_block = row_scale * jnp.clip(jax.random.normal(jax.random.fold_in(base_offset, 2), query_shape, jnp.float32), -6.0, 6.0)
    return (key_cache_store, query_tile_block)


def draw_queries(key, part):
    return joint_draw(key)[1].astype(jnp.bfloat16)


def draw_prompt_key_cache(key, part):
    return joint_draw(key)[0].astype(jnp.bfloat16)


def draw_kept(key, part):
    base_offset = jax.random.fold_in(key, 202)
    kept_block_counts = jax.random.randint(jax.random.fold_in(base_offset, 1), (PROMPT_COUNT, KEY_VALUE_HEADS, N_SEQ), 1, KEPT_SLOTS + 1)
    fullest_count = jax.random.randint(jax.random.fold_in(base_offset, 2), (PROMPT_COUNT, KEY_VALUE_HEADS), 0, N_SEQ)
    device_ids = jnp.arange(N_SEQ, dtype=jnp.int32)
    return jnp.where(device_ids[None, None, :] == fullest_count[:, :, None], KEPT_SLOTS, kept_block_counts).astype(jnp.int32)


def draw_suffix_len(key, part):
    base_offset = jax.random.fold_in(key, 303)
    lengths = jax.random.randint(jax.random.fold_in(base_offset, 1), (PROMPT_COUNT, SAMPLE_COUNT), 1, SUFFIX_LENGTH + 1)
    longest = jax.random.randint(jax.random.fold_in(base_offset, 2), (PROMPT_COUNT,), 0, SAMPLE_COUNT)
    sample_ids = jnp.arange(SAMPLE_COUNT, dtype=jnp.int32)
    return jnp.where(sample_ids[None, :] == longest[:, None], SUFFIX_LENGTH, lengths).astype(jnp.int32)


def shard_levels(stream_key, extent, split, least, top_value):
    factor_of, own = 1.0, jax.random.fold_in(stream_key, 6)
    for dim, blocks in split:
        heights = jnp.exp(jax.random.uniform(jax.random.fold_in(own, dim), (blocks,), jnp.float32, least / len(split), top_value / len(split)))
        factor_of = factor_of * jnp.repeat(heights, extent[dim] // blocks).reshape([-1 if axis == dim else 1 for axis in range(len(extent))])
    return factor_of


def scatter_about(own_key, extent, spread, bound, cuts=(), held_as=jnp.bfloat16):
    result = jax.random.normal(own_key, extent, jnp.float32) * spread
    if len(cuts) > 0:
        result = shard_levels(own_key, extent, cuts, -0.22, 0.18) * result
    return jnp.clip(result, min=-bound, max=bound).astype(held_as)


def setup_inputs(seed: int = 0) -> dict:
    streams_of = jax.random.split(jax.random.key(seed), 11)
    return {
        "queries": draw_queries(jax.random.fold_in(streams_of[10], 71), 0),
        "prompt_key_cache": draw_prompt_key_cache(jax.random.fold_in(streams_of[10], 71), 0),
        "prompt_value_cache": scatter_about(streams_of[2], (PROMPT_COUNT, KEY_VALUE_HEADS, PROMPT_LENGTH, HEAD_SIZE), 1.0, 6.0, ((0, 4), (2, 8))),
        "kept": draw_kept(jax.random.fold_in(streams_of[10], 71), 0),
        "sample_keys": scatter_about(streams_of[4], (PROMPT_COUNT, SAMPLE_COUNT, KEY_VALUE_HEADS, SUFFIX_LENGTH, HEAD_SIZE), 1.3, 6.0, ((0, 4), (1, 8))),
        "sample_values": scatter_about(streams_of[5], (PROMPT_COUNT, SAMPLE_COUNT, KEY_VALUE_HEADS, SUFFIX_LENGTH, HEAD_SIZE), 1.0, 6.0, ((0, 4), (1, 8))),
        "suffix_len": draw_suffix_len(jax.random.fold_in(streams_of[10], 71), 0),
        "decode_keys": scatter_about(streams_of[7], (PROMPT_COUNT, SAMPLE_COUNT, DECODE_STEPS, KEY_VALUE_HEADS, HEAD_SIZE), 1.3, 6.0, ((0, 4), (1, 8))),
        "decode_values": scatter_about(streams_of[8], (PROMPT_COUNT, SAMPLE_COUNT, DECODE_STEPS, KEY_VALUE_HEADS, HEAD_SIZE), 1.0, 6.0, ((0, 4), (1, 8))),
        "out_weight": scatter_about(streams_of[9], (HQ * HEAD_SIZE, D), (HQ * HEAD_SIZE // 4) ** -0.5, 0.1875, ((0, 8), (1, 4))),
    }


NEGATIVE = -1e+30

def rounded_length(values):
    return lax.optimization_barrier(values.astype(jnp.bfloat16)).astype(jnp.float32)

def reference(queries, prompt_key_cache, prompt_value_cache, kept, sample_keys, sample_values, suffix_len, decode_keys, decode_values, out_weight):
    logit_scale = 1.0 / math.sqrt(HEAD_SIZE)
    block_total = N_SEQ * KEPT_SLOTS

    def one_prompt(prompt_position):
        query_tile_block = queries[prompt_position].astype(jnp.float32)
        grouped_queries = query_tile_block.reshape(SAMPLE_COUNT, DECODE_STEPS, KEY_VALUE_HEADS, QUERY_GROUP, HEAD_SIZE)
        heads_leading = jnp.transpose(grouped_queries, (2, 0, 1, 3, 4)).reshape(KEY_VALUE_HEADS, SAMPLE_COUNT * DECODE_STEPS * QUERY_GROUP, HEAD_SIZE)
        key_cache_store = prompt_key_cache[prompt_position].astype(jnp.float32).reshape(KEY_VALUE_HEADS, block_total, BLOCK_TOKENS, HEAD_SIZE)
        value_cache_store = prompt_value_cache[prompt_position].astype(jnp.float32).reshape(KEY_VALUE_HEADS, block_total, BLOCK_TOKENS, HEAD_SIZE)
        slot_position = jnp.arange(KEPT_SLOTS, dtype=jnp.int32)
        active_mask = (slot_position[None, None, :] < kept[prompt_position][:, :, None]).reshape(KEY_VALUE_HEADS, block_total)

        def one_head(pieces):
            head_row_block, key_block_list, value_block_list, live_blocks = pieces
            logit_scores = jnp.einsum('eg,mxg->emx', head_row_block, key_block_list) * logit_scale
            block_max = jnp.where(live_blocks[None, :], lax.optimization_barrier(jnp.max(logit_scores, axis=2)), NEGATIVE)
            attention_weights = jnp.where(live_blocks[None, :, None], jnp.exp(logit_scores - block_max[:, :, None]), 0.0)
            block_sum = lax.optimization_barrier(jnp.sum(attention_weights, axis=2))
            block_output = jnp.einsum('yaf,afi->yai', rounded_length(attention_weights), value_block_list)
            highest = lax.optimization_barrier(jnp.max(block_max, axis=1))
            factor = jnp.exp(block_max - highest[:, None])
            return (highest, lax.optimization_barrier(jnp.sum(factor * block_sum, axis=1)), lax.optimization_barrier(jnp.sum(factor[:, :, None] * block_output, axis=1)))
        prompt_maximum, prompt_sum, prompt_output = lax.map(one_head, (heads_leading, key_cache_store, value_cache_store, active_mask))
        suffix_keys = sample_keys[prompt_position].astype(jnp.float32)
        fresh_keys = jnp.transpose(decode_keys[prompt_position].astype(jnp.float32), (0, 2, 1, 3))
        all_keys = jnp.concatenate([suffix_keys, fresh_keys], axis=2)
        suffix_values = sample_values[prompt_position].astype(jnp.float32)
        fresh_values = jnp.transpose(decode_values[prompt_position].astype(jnp.float32), (0, 2, 1, 3))
        all_values = jnp.concatenate([suffix_values, fresh_values], axis=2)
        logit_scores = jnp.einsum('nthgd,nhid->nhtgi', grouped_queries, all_keys) * logit_scale
        position = jnp.arange(SUFFIX_LENGTH, dtype=jnp.int32)
        sample_token_mask = position[None, :] < suffix_len[prompt_position][:, None]
        sample_token_mask = jnp.broadcast_to(sample_token_mask[:, None, None, None, :], (SAMPLE_COUNT, KEY_VALUE_HEADS, DECODE_STEPS, QUERY_GROUP, SUFFIX_LENGTH))
        step_index = jnp.arange(DECODE_STEPS, dtype=jnp.int32)
        newest_token_mask = step_index[None, :] <= step_index[:, None]
        newest_token_mask = jnp.broadcast_to(newest_token_mask[None, None, :, None, :], (SAMPLE_COUNT, KEY_VALUE_HEADS, DECODE_STEPS, QUERY_GROUP, DECODE_STEPS))
        full_mask = jnp.concatenate([sample_token_mask, newest_token_mask], axis=4)
        tail_max = lax.optimization_barrier(jnp.max(jnp.where(full_mask, logit_scores, NEGATIVE), axis=4))
        attention_weights = jnp.where(full_mask, jnp.exp(logit_scores - tail_max[..., None]), 0.0)
        tail_sum = lax.optimization_barrier(jnp.sum(attention_weights, axis=4))
        tail_out = jnp.einsum('nhtgi,nhid->nhtgd', rounded_length(attention_weights), all_values)
        prefix_maximum = jnp.transpose(prompt_maximum.reshape(KEY_VALUE_HEADS, SAMPLE_COUNT, DECODE_STEPS, QUERY_GROUP), (1, 0, 2, 3))
        prefix_total_sum = jnp.transpose(prompt_sum.reshape(KEY_VALUE_HEADS, SAMPLE_COUNT, DECODE_STEPS, QUERY_GROUP), (1, 0, 2, 3))
        prefix_output = jnp.transpose(prompt_output.reshape(KEY_VALUE_HEADS, SAMPLE_COUNT, DECODE_STEPS, QUERY_GROUP, HEAD_SIZE), (1, 0, 2, 3, 4))
        highest = jnp.maximum(prefix_maximum, tail_max)
        prefix_factor = jnp.exp(prefix_maximum - highest)
        tail_factor = jnp.exp(tail_max - highest)
        softmax_total = prefix_total_sum * prefix_factor + tail_sum * tail_factor
        summed = prefix_output * prefix_factor[..., None] + tail_out * tail_factor[..., None]
        head_values = summed / softmax_total[..., None]
        head_values = jnp.transpose(head_values, (0, 2, 1, 3, 4)).reshape(SAMPLE_COUNT * DECODE_STEPS, HQ * HEAD_SIZE)
        return head_values.astype(jnp.bfloat16)
    head_outputs = lax.map(one_prompt, jnp.arange(PROMPT_COUNT, dtype=jnp.int32))
    flat_rows = head_outputs.reshape(ROWS, HQ * HEAD_SIZE)
    part_width = HQ * HEAD_SIZE // N_SEQ

    def add_group(running, group_index):
        part_rows = lax.dynamic_slice_in_dim(flat_rows, group_index * part_width, part_width, 1)
        part_weight = lax.dynamic_slice_in_dim(out_weight, group_index * part_width, part_width, 0)
        partial_value = jnp.dot(part_rows, part_weight, preferred_element_type=jnp.float32)
        return (running + partial_value, None)
    running, unused = lax.scan(add_group, jnp.zeros((ROWS, D), jnp.float32), jnp.arange(N_SEQ, dtype=jnp.int32))
    return running.astype(jnp.bfloat16)
```

```python
import functools
import math

import jax
import jax.numpy as jnp
from jax import lax
from jax.experimental import pallas as pl
from jax.experimental.pallas import tpu as pltpu
from jax.sharding import PartitionSpec as P

BLOCK_TOKENS = 128
NEGATIVE = -1e30
F32 = jnp.float32
BF16 = jnp.bfloat16
VMEM_LIMIT = 16 * 1024 * 1024
MAX_LANE, SUM_LANE, SUM_REST_LANE, KEPT_LANE = 0, 1, 2, 3


def lanes_of(rows, width, values):
    lane = lax.broadcasted_iota(jnp.int32, (rows, width), 1)
    filled = jnp.zeros((rows, width), F32)
    for i, value in enumerate(values):
        filled = jnp.where(lane == i, value, filled)
    return filled


def dot_rows(a, b):
    return lax.dot_general(a, b, (((1,), (1,)), ((), ())), preferred_element_type=F32)


def message_kernel(
    shape, q_refs, key_ref, value_ref, kept_ref, tail_key_ref, tail_value_ref, len_ref,
    step_key_ref, step_value_ref, out_refs, small,
):
    heads, steps, group, dim, ranks, chunk = shape
    rows = steps * group
    scale = 1.0 / math.sqrt(dim)
    chip = lax.div(lax.axis_index("seq"), ranks)
    for x in range(heads):
        out_refs[x][0:chunk, :] = key_ref[chip ^ x]
        out_refs[x][chunk : 2 * chunk, :] = value_ref[chip ^ x]
    queries = [ref[...].astype(F32) for ref in q_refs]
    step_keys = step_key_ref[...].astype(F32)
    step_values = step_value_ref[...].astype(F32)
    length = len_ref[0]
    position = lax.broadcasted_iota(jnp.int32, (rows, tail_key_ref.shape[1]), 1)
    step_of_row = lax.div(lax.broadcasted_iota(jnp.int32, (rows, 1), 0), group)

    def of_head(whole, h):
        return jnp.concatenate(
            [
                whole[t * heads * group + h * group : t * heads * group + (h + 1) * group]
                for t in range(steps)
            ],
            axis=0,
        )

    for h in range(heads):
        q = of_head(queries[0], h)
        scores = dot_rows(q.astype(BF16), tail_key_ref[h]) * scale
        scores = jnp.where(position < length, scores, NEGATIVE)
        own = []
        for u in range(steps):
            score = jnp.sum(q * step_keys[u, h : h + 1], axis=1, keepdims=True) * scale
            own.append(jnp.where(step_of_row >= u, score, NEGATIVE))
        top = jnp.max(scores, axis=1, keepdims=True)
        for score in own:
            top = jnp.maximum(top, score)
        top = top.astype(BF16).astype(F32)
        weights = jnp.exp(scores - top)
        total = jnp.sum(weights, axis=1, keepdims=True)
        summed = jnp.dot(weights.astype(BF16), tail_value_ref[h], preferred_element_type=F32)
        for u, score in enumerate(own):
            weight = jnp.exp(score - top)
            total = total + weight
            summed = summed + weight.astype(BF16).astype(F32) * step_values[u, h : h + 1]
        summed_high = summed.astype(BF16)
        summed_rest = (summed - summed_high.astype(F32)).astype(BF16)
        total_high = total.astype(BF16).astype(F32)
        kept = kept_ref[h].astype(F32)
        stats = lanes_of(rows, dim, [top, total_high, total - total_high, kept])
        parts = [q.astype(BF16)] + [of_head(other, h).astype(BF16) for other in queries[1:]]
        parts += [summed_high, summed_rest, stats.astype(BF16)]
        for i, part in enumerate(parts):
            small[h, i * rows : (i + 1) * rows, :] = part
    for x in range(heads):
        out_refs[x][2 * chunk :, :] = small[chip ^ x]


def prefix_kernel(shape, message_refs, out_refs, q_all, tails, merged):
    heads, steps, group, dim, ranks, chunk = shape
    rows = steps * group
    local = group // ranks
    scale = 1.0 / math.sqrt(dim)
    me = lax.axis_index("seq")
    chip, rank = lax.div(me, ranks), lax.rem(me, ranks)
    all_rows = q_all.shape[0]
    tails[:, 0:dim] = jnp.zeros((all_rows, dim), F32)
    tails[:, dim:] = lanes_of(all_rows, dim, [NEGATIVE])
    kept = []
    for x in range(heads):
        base = (chip ^ x) * ranks
        start = 2 * chunk
        for y in range(ranks):
            place = pl.multiple_of((base + (rank ^ y)) * rows, rows)
            q_all[pl.ds(place, rows), :] = message_refs[x][start + y * rows : start + (y + 1) * rows, :]
        start += ranks * rows
        place = pl.multiple_of((base + rank) * rows, rows)
        high = message_refs[x][start : start + rows, :].astype(F32)
        rest = message_refs[x][start + rows : start + 2 * rows, :].astype(F32)
        stats = message_refs[x][start + 2 * rows : start + 3 * rows, :].astype(F32)
        tails[pl.ds(place, rows), 0:dim] = high + rest
        total = stats[:, SUM_LANE : SUM_LANE + 1] + stats[:, SUM_REST_LANE : SUM_REST_LANE + 1]
        tails[pl.ds(place, rows), dim:] = lanes_of(
            rows, dim, [stats[:, MAX_LANE : MAX_LANE + 1], total]
        )
        kept.append(stats[0:1, KEPT_LANE : KEPT_LANE + 1])
    block = lax.div(lax.broadcasted_iota(jnp.int32, (1, chunk), 1), BLOCK_TOKENS).astype(F32)
    q = q_all[...]
    tail_top = tails[:, dim + MAX_LANE : dim + MAX_LANE + 1]
    top = tail_top
    scores = []
    for x in range(heads):
        score = dot_rows(q, message_refs[x][0:chunk, :]) * scale
        score = jnp.where(block < kept[x], score, NEGATIVE)
        top = jnp.maximum(top, jnp.max(score, axis=1, keepdims=True))
        scores.append(score)
    factor = jnp.exp(tail_top - top)
    total = tails[:, dim + SUM_LANE : dim + SUM_LANE + 1] * factor
    summed = tails[:, 0:dim] * factor
    for x in range(heads):
        weights = jnp.exp(scores[x] - top)
        total = total + jnp.sum(weights, axis=1, keepdims=True)
        summed = summed + jnp.dot(
            weights.astype(BF16),
            message_refs[x][chunk : 2 * chunk, :],
            preferred_element_type=F32,
        )
    merged[0] = summed
    merged[1] = lanes_of(all_rows, dim, [top, total])
    count = all_rows // group
    for y in range(ranks):
        for i in range(local):
            head = (rank ^ y) * local + i
            for j in range(2):
                out_refs[y][i * count : (i + 1) * count, j * dim : (j + 1) * dim] = merged[
                    j, pl.ds(head, count, stride=group), :
                ]


def merge_kernel(local, part_refs, out_ref):
    dim = out_ref.shape[1] // local
    count = out_ref.shape[0]
    tops = [ref[:, dim + MAX_LANE : dim + MAX_LANE + 1] for ref in part_refs]
    top = functools.reduce(jnp.maximum, tops)
    total, summed = 0.0, 0.0
    for ref, part_top in zip(part_refs, tops):
        factor = jnp.exp(part_top - top)
        total = total + ref[:, dim + SUM_LANE : dim + SUM_LANE + 1] * factor
        summed = summed + ref[:, 0:dim] * factor
    head_out = summed / total
    for i in range(local):
        out_ref[:, i * dim : (i + 1) * dim] = head_out[i * count : (i + 1) * count].astype(BF16)


def project_kernel(heads, ranks, head_refs, weight_ref, out_refs, all_heads, product):
    me = lax.axis_index("seq")
    chip, rank = lax.div(me, ranks), lax.rem(me, ranks)
    prompt = lax.axis_index("prompt")
    count = head_refs[0].shape[0]
    for x, ref in enumerate(head_refs):
        all_heads[pl.ds(pl.multiple_of((prompt ^ x) * count, count), count), :] = ref[...]
    product[...] = jnp.dot(all_heads[...], weight_ref[...], preferred_element_type=F32)
    size = product.shape[0] // (heads * ranks)
    for y in range(ranks):
        pieces = [
            product[pl.ds(pl.multiple_of(((chip ^ x) * ranks + (rank ^ y)) * size, size), size), :]
            for x in range(heads)
        ]
        out_refs[y][...] = jnp.concatenate(pieces, axis=0).astype(out_refs[y].dtype)


def call(kernel, out_shape, in_specs, scratch_shapes=()):
    return pl.pallas_call(
        kernel,
        out_shape=out_shape,
        in_specs=in_specs,
        out_specs=jax.tree.map(lambda _: pl.BlockSpec(memory_space=pltpu.VMEM), out_shape),
        scratch_shapes=scratch_shapes,
        compiler_params=pltpu.CompilerParams(vmem_limit_bytes=VMEM_LIMIT),
    )


def swap(x, axis, distance):
    return lax.ppermute(x, axis, [(i, i ^ distance) for i in range(lax.axis_size(axis))])


def on_device(
    queries,
    prompt_key_cache,
    prompt_value_cache,
    kept,
    sample_keys,
    sample_values,
    suffix_len,
    decode_keys,
    decode_values,
    out_weight,
):
    seq_count, prompt_count = lax.axis_size("seq"), lax.axis_size("prompt")
    steps, head_count, dim = queries.shape[2:]
    heads, chunk = prompt_key_cache.shape[1:3]
    group = head_count // heads
    ranks = seq_count // heads
    local = group // ranks
    shape = (heads, steps, group, dim, ranks, chunk)
    rows = steps * group
    vmem, smem = pl.BlockSpec(memory_space=pltpu.VMEM), pl.BlockSpec(memory_space=pltpu.SMEM)

    own_queries = queries.reshape(steps * head_count, dim)
    rank_queries = [own_queries] + [swap(own_queries, "seq", y) for y in range(1, ranks)]

    small_rows = (ranks + 3) * rows
    message = jax.ShapeDtypeStruct((2 * chunk + small_rows, dim), BF16)

    def run_message(*refs):
        q_refs, refs = refs[:ranks], refs[ranks:]
        message_kernel(shape, q_refs, *refs[:8], refs[8 : 8 + heads], refs[8 + heads])

    messages = call(
        run_message,
        [message] * heads,
        [vmem] * ranks + [vmem, vmem, smem, vmem, vmem, smem, vmem, vmem],
        [pltpu.VMEM((heads, small_rows, dim), BF16)],
    )(
        *rank_queries,
        prompt_key_cache[0],
        prompt_value_cache[0],
        kept.reshape(heads),
        sample_keys[0, 0],
        sample_values[0, 0],
        suffix_len.reshape(1),
        decode_keys[0, 0],
        decode_values[0, 0],
    )
    messages = [messages[0]] + [swap(messages[x], "seq", x * ranks) for x in range(1, heads)]

    all_rows = seq_count * rows
    count = seq_count * steps
    part = jax.ShapeDtypeStruct((local * count, 2 * dim), F32)

    def run_prefix(*refs):
        prefix_kernel(shape, refs[:heads], refs[heads : heads + ranks], *refs[heads + ranks :])

    parts = call(
        run_prefix,
        [part] * ranks,
        [vmem] * heads,
        [
            pltpu.VMEM((all_rows, dim), BF16),
            pltpu.VMEM((all_rows, 2 * dim), F32),
            pltpu.VMEM((2, all_rows, dim), F32),
        ],
    )(*messages)
    parts = [parts[0]] + [swap(parts[y], "seq", y) for y in range(1, ranks)]

    def run_merge(*refs):
        merge_kernel(local, refs[:ranks], refs[ranks])

    head_out = call(
        run_merge, jax.ShapeDtypeStruct((count, local * dim), BF16), [vmem] * ranks
    )(*parts)
    head_outs = [head_out] + [swap(head_out, "prompt", x) for x in range(1, prompt_count)]

    columns = out_weight.shape[1]
    row_count = count * prompt_count
    size = row_count // seq_count

    def run_project(*refs):
        project_kernel(
            heads, ranks, refs[:prompt_count], refs[prompt_count],
            refs[prompt_count + 1 : prompt_count + 1 + ranks], *refs[prompt_count + 1 + ranks :]
        )

    terms = call(
        run_project,
        [jax.ShapeDtypeStruct((heads * size, columns), BF16 if y else F32) for y in range(ranks)],
        [vmem] * (prompt_count + 1),
        [
            pltpu.VMEM((row_count, local * dim), BF16),
            pltpu.VMEM((row_count, columns), F32),
        ],
    )(*head_outs, out_weight)
    total = terms[0]
    for y in range(1, ranks):
        total = total + swap(terms[y], "seq", y).astype(F32)
    total = total.reshape(heads, size, columns)
    result = total[0]
    for x in range(1, heads):
        result = result + swap(total[x].astype(BF16), "seq", x * ranks).astype(F32)
    return result.astype(BF16)


def solution(mesh):
    placed = (
        P("prompt", "seq", None, None, None),
        P("prompt", None, "seq", None),
        P("prompt", None, "seq", None),
        P("prompt", None, "seq"),
        P("prompt", "seq", None, None, None),
        P("prompt", "seq", None, None, None),
        P("prompt", "seq"),
        P("prompt", "seq", None, None, None),
        P("prompt", "seq", None, None, None),
        P("seq", "prompt"),
    )
    return jax.shard_map(
        on_device, mesh=mesh, in_specs=placed, out_specs=P("seq", "prompt"), check_vma=False
    )
```

```python
import functools
import math

import jax
import jax.numpy as jnp
from jax import lax
from jax.experimental import pallas as pl
from jax.experimental.pallas import tpu as pltpu
from jax.sharding import PartitionSpec as P

BLOCK_TOKENS = 128
NEGATIVE = -1e30
F32 = jnp.float32
BF16 = jnp.bfloat16
VMEM_LIMIT = 16 * 1024 * 1024
MAX_LANE, SUM_LANE, SUM_REST_LANE, KEPT_LANE = 0, 1, 2, 3


def lanes_of(rows, width, values):
    lane = lax.broadcasted_iota(jnp.int32, (rows, width), 1)
    filled = jnp.zeros((rows, width), F32)
    for i, value in enumerate(values):
        filled = jnp.where(lane == i, value, filled)
    return filled


def dot_rows(a, b):
    return lax.dot_general(a, b, (((1,), (1,)), ((), ())), preferred_element_type=F32)


def copy_all(pairs, sems):
    copies = [
        pltpu.make_async_copy(source, target, sems.at[i]) for i, (source, target) in enumerate(pairs)
    ]
    for copy in copies:
        copy.start()
    return copies


def message_kernel(shape, in_refs, out_refs, held, small, sems):
    heads, steps, group, dim, ranks, chunk = shape
    rows = steps * group
    scale = 1.0 / math.sqrt(dim)
    chip = lax.div(lax.axis_index("seq"), ranks)
    key_ref, value_ref, *fetched = in_refs
    pairs = list(zip(fetched, held))
    for x in range(heads):
        pairs.append((key_ref.at[chip ^ x], out_refs[x].at[0:chunk]))
        pairs.append((value_ref.at[chip ^ x], out_refs[x].at[chunk : 2 * chunk]))
    copies = [
        pltpu.make_async_copy(source, target, sems.at[i]) for i, (source, target) in enumerate(pairs)
    ]
    for copy in copies:
        copy.start()
    for copy in copies[: len(held)]:
        copy.wait()
    q_ref, tail_key_ref, tail_value_ref, step_key_ref, step_value_ref, kept_ref, len_ref = held
    queries = q_ref[...].astype(F32)
    step_keys = step_key_ref[...].astype(F32)
    step_values = step_value_ref[...].astype(F32)
    length = len_ref[0]
    position = lax.broadcasted_iota(jnp.int32, (rows, tail_key_ref.shape[1]), 1)
    step_of_row = lax.div(lax.broadcasted_iota(jnp.int32, (rows, 1), 0), group)
    for h in range(heads):
        q = rows_of_head(queries, shape, h)
        scores = dot_rows(q.astype(BF16), tail_key_ref[h]) * scale
        scores = jnp.where(position < length, scores, NEGATIVE)
        own = []
        for u in range(steps):
            score = jnp.sum(q * step_keys[u, h : h + 1], axis=1, keepdims=True) * scale
            own.append(jnp.where(step_of_row >= u, score, NEGATIVE))
        top = jnp.max(scores, axis=1, keepdims=True)
        for score in own:
            top = jnp.maximum(top, score)
        top = top.astype(BF16).astype(F32)
        weights = jnp.exp(scores - top)
        total = jnp.sum(weights, axis=1, keepdims=True)
        summed = jnp.dot(weights.astype(BF16), tail_value_ref[h], preferred_element_type=F32)
        for u, score in enumerate(own):
            weight = jnp.exp(score - top)
            total = total + weight
            summed = summed + weight.astype(BF16).astype(F32) * step_values[u, h : h + 1]
        summed_high = summed.astype(BF16)
        summed_rest = (summed - summed_high.astype(F32)).astype(BF16)
        total_high = total.astype(BF16).astype(F32)
        kept = kept_ref[h].astype(F32)
        stats = lanes_of(rows, dim, [top, total_high, total - total_high, kept])
        parts = [summed_high, summed_rest, stats.astype(BF16), q.astype(BF16)]
        for i, part in enumerate(parts):
            small[h, i * rows : (i + 1) * rows, :] = part
    for x in range(heads):
        out_refs[x][2 * chunk : 2 * chunk + 4 * rows, :] = small[chip ^ x]
    for copy in copies[len(held) :]:
        copy.wait()


def rows_of_head(whole, shape, h):
    heads, steps, group, *_ = shape
    return jnp.concatenate(
        [
            whole[(t * heads + h) * group : (t * heads + h + 1) * group]
            for t in range(steps)
        ],
        axis=0,
    )


def query_kernel(shape, q_refs, out_refs, small):
    heads, steps, group, dim, ranks, chunk = shape
    rows = steps * group
    chip = lax.div(lax.axis_index("seq"), ranks)
    for y, ref in enumerate(q_refs):
        queries = ref[...].astype(F32)
        for h in range(heads):
            small[h, y * rows : (y + 1) * rows, :] = rows_of_head(queries, shape, h).astype(BF16)
    start = 2 * chunk + 4 * rows
    for x in range(heads):
        out_refs[x][start : start + len(q_refs) * rows, :] = small[chip ^ x]


def fetch_kernel(after_ref, weight_ref, out_ref, sem):
    copy = pltpu.make_async_copy(weight_ref, out_ref, sem)
    copy.start()
    copy.wait()


def prefix_kernel(shape, message_refs, out_refs, q_all, tails, merged):
    heads, steps, group, dim, ranks, chunk = shape
    rows = steps * group
    local = group // ranks
    scale = 1.0 / math.sqrt(dim)
    me = lax.axis_index("seq")
    chip, rank = lax.div(me, ranks), lax.rem(me, ranks)
    all_rows = q_all.shape[0]
    tails[:, 0:dim] = jnp.zeros((all_rows, dim), F32)
    tails[:, dim:] = lanes_of(all_rows, dim, [NEGATIVE])
    kept = []
    for x in range(heads):
        base = (chip ^ x) * ranks
        start = 2 * chunk
        place = pl.multiple_of((base + rank) * rows, rows)
        high = message_refs[x][start : start + rows, :].astype(F32)
        rest = message_refs[x][start + rows : start + 2 * rows, :].astype(F32)
        stats = message_refs[x][start + 2 * rows : start + 3 * rows, :].astype(F32)
        start += 3 * rows
        for y in range(ranks):
            row = pl.multiple_of((base + (rank ^ y)) * rows, rows)
            q_all[pl.ds(row, rows), :] = message_refs[x][start + y * rows : start + (y + 1) * rows, :]
        tails[pl.ds(place, rows), 0:dim] = high + rest
        total = stats[:, SUM_LANE : SUM_LANE + 1] + stats[:, SUM_REST_LANE : SUM_REST_LANE + 1]
        tails[pl.ds(place, rows), dim:] = lanes_of(
            rows, dim, [stats[:, MAX_LANE : MAX_LANE + 1], total]
        )
        kept.append(stats[0:1, KEPT_LANE : KEPT_LANE + 1])
    block = lax.div(lax.broadcasted_iota(jnp.int32, (1, chunk), 1), BLOCK_TOKENS).astype(F32)
    q = q_all[...]
    tail_top = tails[:, dim + MAX_LANE : dim + MAX_LANE + 1]
    top = tail_top
    scores = []
    for x in range(heads):
        score = dot_rows(q, message_refs[x][0:chunk, :]) * scale
        score = jnp.where(block < kept[x], score, NEGATIVE)
        top = jnp.maximum(top, jnp.max(score, axis=1, keepdims=True))
        scores.append(score)
    factor = jnp.exp(tail_top - top)
    total = tails[:, dim + SUM_LANE : dim + SUM_LANE + 1] * factor
    summed = tails[:, 0:dim] * factor
    for x in range(heads):
        weights = jnp.exp(scores[x] - top)
        total = total + jnp.sum(weights, axis=1, keepdims=True)
        summed = summed + jnp.dot(
            weights.astype(BF16),
            message_refs[x][chunk : 2 * chunk, :],
            preferred_element_type=F32,
        )
    merged[0] = summed
    merged[1] = lanes_of(all_rows, dim, [top, total])
    count = all_rows // group
    for y in range(ranks):
        for i in range(local):
            head = (rank ^ y) * local + i
            for j in range(2):
                out_refs[y][i * count : (i + 1) * count, j * dim : (j + 1) * dim] = merged[
                    j, pl.ds(head, count, stride=group), :
                ]


def merge_kernel(local, part_refs, out_ref):
    dim = out_ref.shape[1] // local
    count = out_ref.shape[0]
    tops = [ref[:, dim + MAX_LANE : dim + MAX_LANE + 1] for ref in part_refs]
    top = functools.reduce(jnp.maximum, tops)
    total, summed = 0.0, 0.0
    for ref, part_top in zip(part_refs, tops):
        factor = jnp.exp(part_top - top)
        total = total + ref[:, dim + SUM_LANE : dim + SUM_LANE + 1] * factor
        summed = summed + ref[:, 0:dim] * factor
    head_out = summed / total
    for i in range(local):
        out_ref[:, i * dim : (i + 1) * dim] = head_out[i * count : (i + 1) * count].astype(BF16)


def project_kernel(heads, ranks, head_refs, weight_ref, out_refs, all_heads, product):
    me = lax.axis_index("seq")
    chip, rank = lax.div(me, ranks), lax.rem(me, ranks)
    prompt = lax.axis_index("prompt")
    count = head_refs[0].shape[0]
    for x, ref in enumerate(head_refs):
        all_heads[pl.ds(pl.multiple_of((prompt ^ x) * count, count), count), :] = ref[...]
    product[...] = jnp.dot(all_heads[...], weight_ref[...], preferred_element_type=F32)
    size = product.shape[0] // (heads * ranks)
    for y in range(ranks):
        pieces = [
            product[pl.ds(pl.multiple_of(((chip ^ x) * ranks + (rank ^ y)) * size, size), size), :]
            for x in range(heads)
        ]
        out_refs[y][...] = jnp.concatenate(pieces, axis=0).astype(out_refs[y].dtype)


def call(kernel, out_shape, in_specs, scratch_shapes=(), aliases=None):
    return pl.pallas_call(
        kernel,
        out_shape=out_shape,
        in_specs=in_specs,
        out_specs=jax.tree.map(lambda _: pl.BlockSpec(memory_space=pltpu.VMEM), out_shape),
        scratch_shapes=scratch_shapes,
        input_output_aliases=aliases or {},
        compiler_params=pltpu.CompilerParams(vmem_limit_bytes=VMEM_LIMIT),
    )


def in_hbm(x):
    return pltpu.with_memory_space_constraint(x, pltpu.HBM)


def swap(x, axis, distance):
    return lax.ppermute(x, axis, [(i, i ^ distance) for i in range(lax.axis_size(axis))])


def on_device(
    queries,
    prompt_key_cache,
    prompt_value_cache,
    kept,
    sample_keys,
    sample_values,
    suffix_len,
    decode_keys,
    decode_values,
    out_weight,
):
    seq_count, prompt_count = lax.axis_size("seq"), lax.axis_size("prompt")
    steps, head_count, dim = queries.shape[2:]
    heads, chunk = prompt_key_cache.shape[1:3]
    group = head_count // heads
    ranks = seq_count // heads
    local = group // ranks
    shape = (heads, steps, group, dim, ranks, chunk)
    rows = steps * group
    vmem = pl.BlockSpec(memory_space=pltpu.VMEM)
    hbm = pl.BlockSpec(memory_space=pltpu.HBM)
    own_queries = queries.reshape(steps * head_count, dim)
    other_queries = [swap(own_queries, "seq", y) for y in range(1, ranks)]

    fetched = [
        own_queries,
        sample_keys[0, 0],
        sample_values[0, 0],
        decode_keys[0, 0],
        decode_values[0, 0],
        kept.reshape(heads),
        suffix_len.reshape(1),
    ]
    sources = [prompt_key_cache[0], prompt_value_cache[0], *fetched]
    message = jax.ShapeDtypeStruct((2 * chunk + (ranks + 3) * rows, dim), BF16)

    def run_message(*refs):
        n, m = len(sources), len(sources) + heads
        message_kernel(shape, refs[:n], refs[n:m], refs[m : m + len(fetched)], *refs[m + len(fetched) :])

    messages = call(
        run_message,
        [message] * heads,
        [hbm] * len(sources),
        [
            (pltpu.SMEM if x.dtype == jnp.int32 else pltpu.VMEM)(x.shape, x.dtype)
            for x in fetched
        ]
        + [
            pltpu.VMEM((heads, 4 * rows, dim), BF16),
            pltpu.SemaphoreType.DMA((len(fetched) + 2 * heads,)),
        ],
    )(*[x if x.dtype == jnp.int32 else in_hbm(x) for x in sources])

    def run_query(*refs):
        n = ranks - 1
        query_kernel(shape, refs[:n], refs[n + heads : n + 2 * heads], refs[-1])

    if ranks > 1:
        messages = call(
            run_query,
            [message] * heads,
            [vmem] * (ranks - 1 + heads),
            [pltpu.VMEM((heads, (ranks - 1) * rows, dim), BF16)],
            {ranks - 1 + x: x for x in range(heads)},
        )(*other_queries, *messages)
    weight = call(
        fetch_kernel,
        jax.ShapeDtypeStruct(out_weight.shape, BF16),
        [pl.BlockSpec(memory_space=pl.ANY), hbm],
        [pltpu.SemaphoreType.DMA(())],
    )(messages[0], in_hbm(out_weight))
    messages = [messages[0]] + [swap(messages[x], "seq", x * ranks) for x in range(1, heads)]

    all_rows = seq_count * rows
    count = seq_count * steps
    part = jax.ShapeDtypeStruct((local * count, 2 * dim), F32)

    def run_prefix(*refs):
        prefix_kernel(shape, refs[:heads], refs[heads : heads + ranks], *refs[heads + ranks :])

    parts = call(
        run_prefix,
        [part] * ranks,
        [vmem] * heads,
        [
            pltpu.VMEM((all_rows, dim), BF16),
            pltpu.VMEM((all_rows, 2 * dim), F32),
            pltpu.VMEM((2, all_rows, dim), F32),
        ],
    )(*messages)
    parts = [parts[0]] + [swap(parts[y], "seq", y) for y in range(1, ranks)]

    def run_merge(*refs):
        merge_kernel(local, refs[:ranks], refs[ranks])

    head_out = call(
        run_merge, jax.ShapeDtypeStruct((count, local * dim), BF16), [vmem] * ranks
    )(*parts)
    head_outs = [head_out] + [swap(head_out, "prompt", x) for x in range(1, prompt_count)]

    columns = out_weight.shape[1]
    row_count = count * prompt_count
    size = row_count // seq_count

    def run_project(*refs):
        project_kernel(
            heads, ranks, refs[:prompt_count], refs[prompt_count],
            refs[prompt_count + 1 : prompt_count + 1 + ranks], *refs[prompt_count + 1 + ranks :]
        )

    terms = call(
        run_project,
        [jax.ShapeDtypeStruct((heads * size, columns), BF16 if y else F32) for y in range(ranks)],
        [vmem] * (prompt_count + 1),
        [
            pltpu.VMEM((row_count, local * dim), BF16),
            pltpu.VMEM((row_count, columns), F32),
        ],
    )(*head_outs, weight)
    total = terms[0]
    for y in range(1, ranks):
        total = total + swap(terms[y], "seq", y).astype(F32)
    total = total.reshape(heads, size, columns)
    result = total[0]
    for x in range(1, heads):
        result = result + swap(total[x].astype(BF16), "seq", x * ranks).astype(F32)
    return result.astype(BF16)


def solution(mesh):
    placed = (
        P("prompt", "seq", None, None, None),
        P("prompt", None, "seq", None),
        P("prompt", None, "seq", None),
        P("prompt", None, "seq"),
        P("prompt", "seq", None, None, None),
        P("prompt", "seq", None, None, None),
        P("prompt", "seq"),
        P("prompt", "seq", None, None, None),
        P("prompt", "seq", None, None, None),
        P("seq", "prompt"),
    )
    return jax.shard_map(
        on_device, mesh=mesh, in_specs=placed, out_specs=P("seq", "prompt"), check_vma=False
    )
```

```python
import functools
import math

import jax
import jax.numpy as jnp
from jax import lax
from jax.experimental import pallas as pl
from jax.experimental.pallas import tpu as pltpu
from jax.sharding import PartitionSpec as P

BLOCK_TOKENS = 128
KEPT_SLOTS = 2
NEGATIVE = -1e30
F32 = jnp.float32
BF16 = jnp.bfloat16
VMEM_LIMIT = 16 * 1024 * 1024
MAX_LANE, SUM_LANE, SUM_REST_LANE, KEPT_LANE = 0, 1, 2, 3


def lanes_of(rows, width, values):
    lane = lax.broadcasted_iota(jnp.int32, (rows, width), 1)
    filled = jnp.zeros((rows, width), F32)
    for i, value in enumerate(values):
        filled = jnp.where(lane == i, value, filled)
    return filled


def dot_rows(a, b):
    return lax.dot_general(a, b, (((1,), (1,)), ((), ())), preferred_element_type=F32)


def copy_all(pairs, sems):
    copies = [
        pltpu.make_async_copy(source, target, sems.at[i]) for i, (source, target) in enumerate(pairs)
    ]
    for copy in copies:
        copy.start()
    return copies


def message_kernel(shape, in_refs, out_refs, held, small, sems):
    heads, steps, group, dim, ranks, chunk = shape
    rows = steps * group
    scale = 1.0 / math.sqrt(dim)
    chip = lax.div(lax.axis_index("seq"), ranks)
    key_ref, value_ref, *fetched = in_refs
    pairs = list(zip(fetched, held))
    for x in range(heads):
        pairs.append((key_ref.at[chip ^ x], out_refs[x].at[0:chunk]))
        pairs.append((value_ref.at[chip ^ x], out_refs[x].at[chunk : 2 * chunk]))
    copies = [
        pltpu.make_async_copy(source, target, sems.at[i]) for i, (source, target) in enumerate(pairs)
    ]
    for copy in copies:
        copy.start()
    for copy in copies[: len(held)]:
        copy.wait()
    q_ref, tail_key_ref, tail_value_ref, step_key_ref, step_value_ref, kept_ref, len_ref = held
    queries = q_ref[...].astype(F32)
    step_keys = step_key_ref[...].astype(F32)
    step_values = step_value_ref[...].astype(F32)
    all_rows = heads * rows
    q = jnp.concatenate([rows_of_head(queries, shape, h) for h in range(heads)], axis=0)
    q_narrow = q.astype(BF16)

    def by_head(x):
        return [x[h * rows : (h + 1) * rows] for h in range(heads)]

    def spread(x):
        return jnp.concatenate([jnp.broadcast_to(x[h : h + 1], (rows, dim)) for h in range(heads)], axis=0)

    scores = jnp.concatenate(
        [dot_rows(part, tail_key_ref[h]) for h, part in enumerate(by_head(q_narrow))], axis=0
    )
    position = lax.broadcasted_iota(jnp.int32, scores.shape, 1)
    scores = jnp.where(position < len_ref[0], scores * scale, NEGATIVE)
    row = lax.broadcasted_iota(jnp.int32, (all_rows, 1), 0)
    step_of_row = lax.rem(lax.div(row, group), steps)
    own = []
    for u in range(steps):
        score = jnp.sum(q * spread(step_keys[u]), axis=1, keepdims=True) * scale
        own.append(jnp.where(step_of_row >= u, score, NEGATIVE))
    top = functools.reduce(jnp.maximum, own, jnp.max(scores, axis=1, keepdims=True))
    top = top.astype(BF16).astype(F32)
    weights = jnp.exp(scores - top)
    total = jnp.sum(weights, axis=1, keepdims=True)
    summed = jnp.concatenate(
        [
            jnp.dot(part, tail_value_ref[h], preferred_element_type=F32)
            for h, part in enumerate(by_head(weights.astype(BF16)))
        ],
        axis=0,
    )
    for u, score in enumerate(own):
        weight = jnp.exp(score - top)
        total = total + weight
        summed = summed + weight.astype(BF16).astype(F32) * spread(step_values[u])
    summed_high = summed.astype(BF16)
    summed_rest = (summed - summed_high.astype(F32)).astype(BF16)
    total_high = total.astype(BF16).astype(F32)
    kept = jnp.concatenate([jnp.full((rows, 1), kept_ref[h].astype(F32)) for h in range(heads)], axis=0)
    stats = lanes_of(all_rows, dim, [top, total_high, total - total_high, kept]).astype(BF16)
    for i, part in enumerate([summed_high, summed_rest, stats, q_narrow]):
        for h, piece in enumerate(by_head(part)):
            small[h, i * rows : (i + 1) * rows, :] = piece
    for x in range(heads):
        out_refs[x][2 * chunk : 2 * chunk + 4 * rows, :] = small[chip ^ x]
    for copy in copies[len(held) :]:
        copy.wait()


def rows_of_head(whole, shape, h):
    heads, steps, group, *_ = shape
    return jnp.concatenate(
        [
            whole[(t * heads + h) * group : (t * heads + h + 1) * group]
            for t in range(steps)
        ],
        axis=0,
    )


def query_kernel(shape, q_refs, out_refs, small):
    heads, steps, group, dim, ranks, chunk = shape
    rows = steps * group
    chip = lax.div(lax.axis_index("seq"), ranks)
    for y, ref in enumerate(q_refs):
        queries = ref[...].astype(F32)
        for h in range(heads):
            small[h, y * rows : (y + 1) * rows, :] = rows_of_head(queries, shape, h).astype(BF16)
    start = 2 * chunk + 4 * rows
    for x in range(heads):
        out_refs[x][start : start + len(q_refs) * rows, :] = small[chip ^ x]


def fetch_kernel(after_ref, weight_ref, out_ref, sem):
    copy = pltpu.make_async_copy(weight_ref, out_ref, sem)
    copy.start()
    copy.wait()


def prefix_kernel(shape, message_refs, out_refs, q_all, tails, merged):
    heads, steps, group, dim, ranks, chunk = shape
    rows = steps * group
    scale = 1.0 / math.sqrt(dim)
    me = lax.axis_index("seq")
    chip, rank = lax.div(me, ranks), lax.rem(me, ranks)
    all_rows = q_all.shape[0]
    tails[:, 0:dim] = jnp.zeros((all_rows, dim), F32)
    tails[:, dim:] = lanes_of(all_rows, dim, [NEGATIVE])
    kept = []
    for x in range(heads):
        base = (chip ^ x) * ranks
        start = 2 * chunk
        place = pl.multiple_of((base + rank) * rows, rows)
        high = message_refs[x][start : start + rows, :].astype(F32)
        rest = message_refs[x][start + rows : start + 2 * rows, :].astype(F32)
        stats = message_refs[x][start + 2 * rows : start + 3 * rows, :].astype(F32)
        start += 3 * rows
        for y in range(ranks):
            row = pl.multiple_of((base + (rank ^ y)) * rows, rows)
            q_all[pl.ds(row, rows), :] = message_refs[x][start + y * rows : start + (y + 1) * rows, :]
        tails[pl.ds(place, rows), 0:dim] = high + rest
        total = stats[:, SUM_LANE : SUM_LANE + 1] + stats[:, SUM_REST_LANE : SUM_REST_LANE + 1]
        tails[pl.ds(place, rows), dim:] = lanes_of(
            rows, dim, [stats[:, MAX_LANE : MAX_LANE + 1], total]
        )
        kept.append(stats[0:1, KEPT_LANE : KEPT_LANE + 1])
    block = lax.div(lax.broadcasted_iota(jnp.int32, (1, chunk), 1), BLOCK_TOKENS).astype(F32)
    q = q_all[...]
    tail_top = tails[:, dim + MAX_LANE : dim + MAX_LANE + 1]
    top = tail_top
    scores = []
    for x in range(heads):
        score = dot_rows(q, message_refs[x][0:chunk, :]) * scale
        score = jnp.where(block < kept[x], score, NEGATIVE)
        top = jnp.maximum(top, jnp.max(score, axis=1, keepdims=True))
        scores.append(score)
    factor = jnp.exp(tail_top - top)
    total = tails[:, dim + SUM_LANE : dim + SUM_LANE + 1] * factor
    summed = tails[:, 0:dim] * factor
    for x in range(heads):
        weights = jnp.exp(scores[x] - top)
        total = total + jnp.sum(weights, axis=1, keepdims=True)
        summed = summed + jnp.dot(
            weights.astype(BF16),
            message_refs[x][chunk : 2 * chunk, :],
            preferred_element_type=F32,
        )
    merged[:, 0:dim] = summed
    merged[:, dim:] = lanes_of(all_rows, dim, [top, total])
    block = all_rows // ranks
    for y in range(ranks):
        out_refs[y][...] = merged[pl.ds(pl.multiple_of((rank ^ y) * block, block), block), :]


def merge_kernel(group, part_refs, out_ref, merged):
    dim = out_ref.shape[1] // group
    tops = [ref[:, dim + MAX_LANE : dim + MAX_LANE + 1] for ref in part_refs]
    top = functools.reduce(jnp.maximum, tops)
    total, summed = 0.0, 0.0
    for ref, part_top in zip(part_refs, tops):
        factor = jnp.exp(part_top - top)
        total = total + ref[:, dim + SUM_LANE : dim + SUM_LANE + 1] * factor
        summed = summed + ref[:, 0:dim] * factor
    merged[...] = summed / total
    count = out_ref.shape[0]
    for g in range(group):
        out_ref[:, g * dim : (g + 1) * dim] = merged[pl.ds(g, count, stride=group), :].astype(BF16)


def project_kernel(ranks, head_refs, weight_refs, out_refs, all_heads):
    me = lax.axis_index("seq")
    chip, rank = lax.div(me, ranks), lax.rem(me, ranks)
    prompt = lax.axis_index("prompt")
    count = head_refs[0].shape[0]
    for x, ref in enumerate(head_refs):
        place = pl.multiple_of((chip ^ prompt ^ x) * count, count)
        all_heads[pl.ds(place, count), :] = ref[...].astype(F32)
    depth = weight_refs[0].shape[0]
    product = 0.0
    for y, ref in enumerate(weight_refs):
        columns = pl.ds(pl.multiple_of((rank ^ y) * depth, depth), depth)
        product = product + jnp.dot(
            all_heads[:, columns].astype(BF16), ref[...], preferred_element_type=F32
        )
    for x, ref in enumerate(out_refs):
        ref[...] = product[x * count : (x + 1) * count].astype(ref.dtype)


def call(kernel, out_shape, in_specs, scratch_shapes=(), aliases=None):
    return pl.pallas_call(
        kernel,
        out_shape=out_shape,
        in_specs=in_specs,
        out_specs=jax.tree.map(lambda _: pl.BlockSpec(memory_space=pltpu.VMEM), out_shape),
        scratch_shapes=scratch_shapes,
        input_output_aliases=aliases or {},
        compiler_params=pltpu.CompilerParams(vmem_limit_bytes=VMEM_LIMIT),
    )


def in_hbm(x):
    return pltpu.with_memory_space_constraint(x, pltpu.HBM)


def swap(x, axis, distance):
    return lax.ppermute(x, axis, [(i, i ^ distance) for i in range(lax.axis_size(axis))])


def joined(x, axis, combine):
    everything = jax.tree.map(lambda part: lax.all_gather(part, axis), x)
    initial = jax.tree.map(lambda part: part[0], everything)

    def lap(k, so_far):
        return combine(so_far, jax.tree.map(lambda part: part[k], everything))

    return lax.fori_loop(1, lax.axis_size(axis), lap, initial)


def combine(earlier, later):
    highest = jnp.maximum(earlier[0], later[0])
    early_factor = jnp.exp(earlier[0] - highest)
    late_factor = jnp.exp(later[0] - highest)
    softmax_total = earlier[1] * early_factor + later[1] * late_factor
    summed = earlier[2] * early_factor[..., None] + later[2] * late_factor[..., None]
    return (highest, softmax_total, summed)


def general_path(
    queries,
    prompt_key_cache,
    prompt_value_cache,
    kept,
    sample_keys,
    sample_values,
    suffix_len,
    decode_keys,
    decode_values,
    out_weight,
):
    seq_count = lax.axis_size("seq")
    seq_index = lax.axis_index("seq")
    own_count = queries.shape[1]
    step_count = queries.shape[2]
    head_count = queries.shape[3]
    head_dim = queries.shape[4]
    kv_count = prompt_key_cache.shape[1]
    group_size = head_count // kv_count
    logit_scale = 1.0 / math.sqrt(head_dim)
    gathered = lax.all_gather(queries, "seq", axis=1, tiled=True)
    sample_count = gathered.shape[1]
    grouped_queries = gathered[0].reshape(sample_count, step_count, kv_count, group_size, head_dim)
    query_rows = jnp.transpose(grouped_queries, (2, 0, 1, 3, 4)).reshape(
        kv_count, sample_count * step_count * group_size, head_dim
    )
    key_cache_store = prompt_key_cache[0].reshape(kv_count, KEPT_SLOTS, BLOCK_TOKENS, head_dim)
    value_cache_store = prompt_value_cache[0].reshape(kv_count, KEPT_SLOTS, BLOCK_TOKENS, head_dim)
    kept_block_counts = kept[0, :, 0]
    active_mask = jnp.arange(KEPT_SLOTS, dtype=jnp.int32)[None, :] < kept_block_counts[:, None]

    def one_head(pieces):
        head_row_block, key_block_list, value_block_list, live_blocks = pieces
        logit_scores = (
            jnp.einsum(
                "eg,mxg->emx", head_row_block, key_block_list, preferred_element_type=jnp.float32
            )
            * logit_scale
        )
        block_max = jnp.where(live_blocks[None, :], jnp.max(logit_scores, axis=2), NEGATIVE)
        attention_weights = jnp.where(
            live_blocks[None, :, None], jnp.exp(logit_scores - block_max[:, :, None]), 0.0
        )
        block_sum = jnp.sum(attention_weights, axis=2)
        block_output = jnp.einsum(
            "yaf,afi->yai",
            attention_weights.astype(jnp.bfloat16),
            value_block_list,
            preferred_element_type=jnp.float32,
        )
        highest = jnp.max(block_max, axis=1)
        factor = jnp.exp(block_max - highest[:, None])
        return (
            highest,
            jnp.sum(factor * block_sum, axis=1),
            jnp.sum(factor[:, :, None] * block_output, axis=1),
        )

    prompt_maximum, prompt_sum, prompt_output = lax.map(
        one_head, (query_rows, key_cache_store, value_cache_store, active_mask)
    )
    own_queries = queries[0].reshape(own_count, step_count, kv_count, group_size, head_dim)
    suffix_scores = (
        jnp.einsum(
            "nthgd,nhid->nhtgi", own_queries, sample_keys[0], preferred_element_type=jnp.float32
        )
        * logit_scale
    )
    fresh_scores = (
        jnp.einsum(
            "nthgd,nuhd->nhtgu", own_queries, decode_keys[0], preferred_element_type=jnp.float32
        )
        * logit_scale
    )
    position = jnp.arange(sample_keys.shape[3], dtype=jnp.int32)
    sample_token_mask = (position[None, :] < suffix_len[0][:, None])[:, None, None, None, :]
    step_index = jnp.arange(step_count, dtype=jnp.int32)
    newest_token_mask = (step_index[None, :] <= step_index[:, None])[None, None, :, None, :]
    tail_max = jnp.maximum(
        jnp.max(jnp.where(sample_token_mask, suffix_scores, NEGATIVE), axis=4),
        jnp.max(jnp.where(newest_token_mask, fresh_scores, NEGATIVE), axis=4),
    )
    suffix_weights = jnp.where(sample_token_mask, jnp.exp(suffix_scores - tail_max[..., None]), 0.0)
    fresh_weights = jnp.where(newest_token_mask, jnp.exp(fresh_scores - tail_max[..., None]), 0.0)
    tail_sum = jnp.sum(suffix_weights, axis=4) + jnp.sum(fresh_weights, axis=4)
    tail_out = jnp.einsum(
        "nhtgi,nhid->nhtgd",
        suffix_weights.astype(jnp.bfloat16),
        sample_values[0],
        preferred_element_type=jnp.float32,
    )
    tail_out = tail_out + jnp.einsum(
        "nhtgu,nuhd->nhtgd",
        fresh_weights.astype(jnp.bfloat16),
        decode_values[0],
        preferred_element_type=jnp.float32,
    )
    tail_part = (
        jnp.transpose(tail_max, (1, 0, 2, 3)),
        jnp.transpose(tail_sum, (1, 0, 2, 3)),
        jnp.transpose(tail_out, (1, 0, 2, 3, 4)),
    )
    prefix = (
        prompt_maximum.reshape(kv_count, sample_count, step_count, group_size),
        prompt_sum.reshape(kv_count, sample_count, step_count, group_size),
        prompt_output.reshape(kv_count, sample_count, step_count, group_size, head_dim),
    )
    offset = seq_index * own_count
    own_part = tuple((lax.dynamic_slice_in_dim(member, offset, own_count, 1) for member in prefix))
    merged = combine(own_part, tail_part)
    prefix = tuple(
        (
            lax.dynamic_update_slice_in_dim(member, update, offset, 1)
            for member, update in zip(prefix, merged)
        )
    )
    part_max = jnp.transpose(prefix[0], (1, 2, 0, 3)).reshape(sample_count, step_count, head_count)
    part_total = jnp.transpose(prefix[1], (1, 2, 0, 3)).reshape(
        sample_count, step_count, head_count
    )
    part_out = jnp.transpose(prefix[2], (1, 2, 0, 3, 4)).reshape(
        sample_count, step_count, head_count, head_dim
    )
    local_heads = head_count // seq_count
    highest, softmax_total, summed = joined((part_max, part_total, part_out), "seq", combine)
    highest = lax.dynamic_slice_in_dim(highest, seq_index * local_heads, local_heads, 2)
    softmax_total = lax.dynamic_slice_in_dim(softmax_total, seq_index * local_heads, local_heads, 2)
    summed = lax.dynamic_slice_in_dim(summed, seq_index * local_heads, local_heads, 2)
    head_out = (
        (summed / softmax_total[..., None])
        .astype(jnp.bfloat16)
        .reshape(sample_count * step_count, local_heads * head_dim)
    )
    all_rows = lax.all_gather(head_out, "prompt", axis=0, tiled=True)
    result = lax.psum_scatter(
        jnp.dot(all_rows, out_weight, preferred_element_type=jnp.float32),
        "seq",
        scatter_dimension=0,
        tiled=True,
    )
    return result.astype(jnp.bfloat16)


def on_device(
    queries,
    prompt_key_cache,
    prompt_value_cache,
    kept,
    sample_keys,
    sample_values,
    suffix_len,
    decode_keys,
    decode_values,
    out_weight,
):
    seq_count, prompt_count = lax.axis_size("seq"), lax.axis_size("prompt")
    if prompt_count != prompt_key_cache.shape[1]:
        return general_path(
            queries, prompt_key_cache, prompt_value_cache, kept, sample_keys, sample_values,
            suffix_len, decode_keys, decode_values, out_weight,
        )
    steps, head_count, dim = queries.shape[2:]
    heads, chunk = prompt_key_cache.shape[1:3]
    group = head_count // heads
    ranks = seq_count // heads
    shape = (heads, steps, group, dim, ranks, chunk)
    rows = steps * group
    vmem = pl.BlockSpec(memory_space=pltpu.VMEM)
    hbm = pl.BlockSpec(memory_space=pltpu.HBM)
    own_queries = queries.reshape(steps * head_count, dim)
    other_queries = [swap(own_queries, "seq", y) for y in range(1, ranks)]

    fetched = [
        own_queries,
        sample_keys[0, 0],
        sample_values[0, 0],
        decode_keys[0, 0],
        decode_values[0, 0],
        kept.reshape(heads),
        suffix_len.reshape(1),
    ]
    sources = [prompt_key_cache[0], prompt_value_cache[0], *fetched]
    message = jax.ShapeDtypeStruct((2 * chunk + (ranks + 3) * rows, dim), BF16)

    def run_message(*refs):
        n, m = len(sources), len(sources) + heads
        message_kernel(shape, refs[:n], refs[n:m], refs[m : m + len(fetched)], *refs[m + len(fetched) :])

    messages = call(
        run_message,
        [message] * heads,
        [hbm] * len(sources),
        [
            (pltpu.SMEM if x.dtype == jnp.int32 else pltpu.VMEM)(x.shape, x.dtype)
            for x in fetched
        ]
        + [
            pltpu.VMEM((heads, 4 * rows, dim), BF16),
            pltpu.SemaphoreType.DMA((len(fetched) + 2 * heads,)),
        ],
    )(*[x if x.size == 1 else in_hbm(x) for x in sources])

    def run_query(*refs):
        n = ranks - 1
        query_kernel(shape, refs[:n], refs[n + heads : n + 2 * heads], refs[-1])

    if ranks > 1:
        messages = call(
            run_query,
            [message] * heads,
            [vmem] * (ranks - 1 + heads),
            [pltpu.VMEM((heads, (ranks - 1) * rows, dim), BF16)],
            {ranks - 1 + x: x for x in range(heads)},
        )(*other_queries, *messages)
    late_weight, messages = lax.optimization_barrier((out_weight, messages))
    other_weights = [swap(late_weight, "seq", y) for y in range(1, ranks)]
    weight = call(
        fetch_kernel,
        jax.ShapeDtypeStruct(out_weight.shape, BF16),
        [pl.BlockSpec(memory_space=pl.ANY), hbm],
        [pltpu.SemaphoreType.DMA(())],
    )(messages[0], in_hbm(out_weight))
    messages = [messages[0]] + [swap(messages[x], "seq", x * ranks) for x in range(1, heads)]

    all_rows = seq_count * rows
    block = all_rows // ranks
    part = jax.ShapeDtypeStruct((block, 2 * dim), F32)

    def run_prefix(*refs):
        prefix_kernel(shape, refs[:heads], refs[heads : heads + ranks], *refs[heads + ranks :])

    parts = call(
        run_prefix,
        [part] * ranks,
        [vmem] * heads,
        [
            pltpu.VMEM((all_rows, dim), BF16),
            pltpu.VMEM((all_rows, 2 * dim), F32),
            pltpu.VMEM((all_rows, 2 * dim), F32),
        ],
    )(*messages)
    parts = [parts[0]] + [swap(parts[y], "seq", y) for y in range(1, ranks)]

    def run_merge(*refs):
        merge_kernel(group, refs[:ranks], *refs[ranks:])

    count = block // group
    head_out = call(
        run_merge,
        jax.ShapeDtypeStruct((count, group * dim), BF16),
        [vmem] * ranks,
        [pltpu.VMEM((block, dim), F32)],
    )(*parts)
    head_outs = [head_out] + [swap(head_out, "prompt", x) for x in range(1, prompt_count)]

    def run_project(*refs):
        n, m = prompt_count, prompt_count + ranks
        project_kernel(ranks, refs[:n], refs[n:m], refs[m : m + heads], refs[m + heads])

    terms = call(
        run_project,
        [
            jax.ShapeDtypeStruct((count, out_weight.shape[1]), BF16 if x else F32)
            for x in range(heads)
        ],
        [vmem] * (prompt_count + ranks),
        [pltpu.VMEM((prompt_count * count, group * dim), F32)],
    )(*head_outs, weight, *other_weights)
    result = terms[0]
    for x in reversed(range(1, heads)):
        result = result + swap(terms[x], "seq", x * ranks).astype(F32)
    return result.astype(BF16)


def solution(mesh):
    placed = (
        P("prompt", "seq", None, None, None),
        P("prompt", None, "seq", None),
        P("prompt", None, "seq", None),
        P("prompt", None, "seq"),
        P("prompt", "seq", None, None, None),
        P("prompt", "seq", None, None, None),
        P("prompt", "seq"),
        P("prompt", "seq", None, None, None),
        P("prompt", "seq", None, None, None),
        P("seq", "prompt"),
    )
    return jax.shard_map(
        on_device, mesh=mesh, in_specs=placed, out_specs=P("seq", "prompt"), check_vma=False
    )
```

```python
import functools
import math

import jax
import jax.numpy as jnp
from jax import lax
from jax.experimental import pallas as pl
from jax.experimental.pallas import tpu as pltpu
from jax.sharding import PartitionSpec as P

BLOCK_TOKENS = 128
KEPT_SLOTS = 2
NEGATIVE = -1e30
F32 = jnp.float32
BF16 = jnp.bfloat16
VMEM_LIMIT = 16 * 1024 * 1024
MAX_LANE, SUM_LANE, SUM_REST_LANE, KEPT_LANE = 0, 1, 2, 3


def lanes_of(rows, width, values):
    lane = lax.broadcasted_iota(jnp.int32, (rows, width), 1)
    filled = jnp.zeros((rows, width), F32)
    for i, value in enumerate(values):
        filled = jnp.where(lane == i, value, filled)
    return filled


def dot_rows(a, b):
    return lax.dot_general(a, b, (((1,), (1,)), ((), ())), preferred_element_type=F32)


def copy_all(pairs, sems):
    copies = [
        pltpu.make_async_copy(source, target, sems.at[i]) for i, (source, target) in enumerate(pairs)
    ]
    for copy in copies:
        copy.start()
    return copies


def message_kernel(shape, in_refs, out_refs, held, small, sems):
    heads, steps, group, dim, ranks, chunk = shape
    rows = steps * group
    scale = 1.0 / math.sqrt(dim)
    chip = lax.div(lax.axis_index("seq"), ranks)
    key_ref, value_ref, *fetched = in_refs
    pairs = list(zip(fetched, held))
    for x in range(heads):
        pairs.append((key_ref.at[chip ^ x], out_refs[x].at[0:chunk]))
        pairs.append((value_ref.at[chip ^ x], out_refs[x].at[chunk : 2 * chunk]))
    copies = [
        pltpu.make_async_copy(source, target, sems.at[i]) for i, (source, target) in enumerate(pairs)
    ]
    for copy in copies:
        copy.start()
    for copy in copies[: len(held)]:
        copy.wait()
    q_ref, tail_key_ref, tail_value_ref, step_key_ref, step_value_ref, kept_ref, len_ref = held
    queries = q_ref[...].astype(F32)
    step_keys = step_key_ref[...].astype(F32)
    step_values = step_value_ref[...].astype(F32)
    all_rows = heads * rows
    q = jnp.concatenate([rows_of_head(queries, shape, h) for h in range(heads)], axis=0)
    q_narrow = q.astype(BF16)

    def by_head(x):
        return [x[h * rows : (h + 1) * rows] for h in range(heads)]

    def spread(x):
        return jnp.concatenate([jnp.broadcast_to(x[h : h + 1], (rows, dim)) for h in range(heads)], axis=0)

    scores = jnp.concatenate(
        [dot_rows(part, tail_key_ref[h]) for h, part in enumerate(by_head(q_narrow))], axis=0
    )
    position = lax.broadcasted_iota(jnp.int32, scores.shape, 1)
    scores = jnp.where(position < len_ref[0], scores * scale, NEGATIVE)
    row = lax.broadcasted_iota(jnp.int32, (all_rows, 1), 0)
    step_of_row = lax.rem(lax.div(row, group), steps)
    own = []
    for u in range(steps):
        score = jnp.sum(q * spread(step_keys[u]), axis=1, keepdims=True) * scale
        own.append(jnp.where(step_of_row >= u, score, NEGATIVE))
    top = functools.reduce(jnp.maximum, own, jnp.max(scores, axis=1, keepdims=True))
    top = top.astype(BF16).astype(F32)
    weights = jnp.exp(scores - top)
    total = jnp.sum(weights, axis=1, keepdims=True)
    summed = jnp.concatenate(
        [
            jnp.dot(part, tail_value_ref[h], preferred_element_type=F32)
            for h, part in enumerate(by_head(weights.astype(BF16)))
        ],
        axis=0,
    )
    for u, score in enumerate(own):
        weight = jnp.exp(score - top)
        total = total + weight
        summed = summed + weight.astype(BF16).astype(F32) * spread(step_values[u])
    summed_high = summed.astype(BF16)
    summed_rest = (summed - summed_high.astype(F32)).astype(BF16)
    total_high = total.astype(BF16).astype(F32)
    kept = jnp.concatenate([jnp.full((rows, 1), kept_ref[h].astype(F32)) for h in range(heads)], axis=0)
    stats = lanes_of(all_rows, dim, [top, total_high, total - total_high, kept]).astype(BF16)
    for i, part in enumerate([summed_high, summed_rest, stats, q_narrow]):
        for h, piece in enumerate(by_head(part)):
            small[h, i * rows : (i + 1) * rows, :] = piece
    for x in range(heads):
        out_refs[x][2 * chunk : 2 * chunk + 4 * rows, :] = small[chip ^ x]
    for copy in copies[len(held) :]:
        copy.wait()


def rows_of_head(whole, shape, h):
    heads, steps, group, *_ = shape
    return jnp.concatenate(
        [
            whole[(t * heads + h) * group : (t * heads + h + 1) * group]
            for t in range(steps)
        ],
        axis=0,
    )


def query_kernel(shape, q_refs, out_refs, small):
    heads, steps, group, dim, ranks, chunk = shape
    rows = steps * group
    chip = lax.div(lax.axis_index("seq"), ranks)
    for y, ref in enumerate(q_refs):
        queries = ref[...].astype(F32)
        for h in range(heads):
            small[h, y * rows : (y + 1) * rows, :] = rows_of_head(queries, shape, h).astype(BF16)
    start = 2 * chunk + 4 * rows
    for x in range(heads):
        out_refs[x][start : start + len(q_refs) * rows, :] = small[chip ^ x]


def fetch_kernel(after_ref, weight_ref, out_ref, sem):
    copy = pltpu.make_async_copy(weight_ref, out_ref, sem)
    copy.start()
    copy.wait()


def prefix_kernel(shape, message_refs, out_ref, q_all, tails):
    heads, steps, group, dim, ranks, chunk = shape
    rows = steps * group
    scale = 1.0 / math.sqrt(dim)
    me = lax.axis_index("seq")
    chip, rank = lax.div(me, ranks), lax.rem(me, ranks)
    all_rows = q_all.shape[0]
    tails[:, 0:dim] = jnp.zeros((all_rows, dim), F32)
    tails[:, dim:] = lanes_of(all_rows, dim, [NEGATIVE])
    kept = []
    for x in range(heads):
        base = (chip ^ x) * ranks
        start = 2 * chunk
        place = pl.multiple_of((base + rank) * rows, rows)
        high = message_refs[x][start : start + rows, :].astype(F32)
        rest = message_refs[x][start + rows : start + 2 * rows, :].astype(F32)
        stats = message_refs[x][start + 2 * rows : start + 3 * rows, :].astype(F32)
        start += 3 * rows
        for y in range(ranks):
            row = pl.multiple_of((base + (rank ^ y)) * rows, rows)
            q_all[pl.ds(row, rows), :] = message_refs[x][start + y * rows : start + (y + 1) * rows, :]
        tails[pl.ds(place, rows), 0:dim] = high + rest
        total = stats[:, SUM_LANE : SUM_LANE + 1] + stats[:, SUM_REST_LANE : SUM_REST_LANE + 1]
        tails[pl.ds(place, rows), dim:] = lanes_of(
            rows, dim, [stats[:, MAX_LANE : MAX_LANE + 1], total]
        )
        kept.append(stats[0:1, KEPT_LANE : KEPT_LANE + 1])
    block = lax.div(lax.broadcasted_iota(jnp.int32, (1, chunk), 1), BLOCK_TOKENS).astype(F32)
    q = q_all[...]
    tail_top = tails[:, dim + MAX_LANE : dim + MAX_LANE + 1]
    top = tail_top
    scores = []
    for x in range(heads):
        score = dot_rows(q, message_refs[x][0:chunk, :]) * scale
        score = jnp.where(block < kept[x], score, NEGATIVE)
        top = jnp.maximum(top, jnp.max(score, axis=1, keepdims=True))
        scores.append(score)
    factor = jnp.exp(tail_top - top)
    total = tails[:, dim + SUM_LANE : dim + SUM_LANE + 1] * factor
    summed = tails[:, 0:dim] * factor
    for x in range(heads):
        weights = jnp.exp(scores[x] - top)
        total = total + jnp.sum(weights, axis=1, keepdims=True)
        summed = summed + jnp.dot(
            weights.astype(BF16),
            message_refs[x][chunk : 2 * chunk, :],
            preferred_element_type=F32,
        )
    out_ref[:, 0:dim] = summed
    out_ref[:, dim:] = lanes_of(all_rows, dim, [top, total])


def block_of(rank, chip, prompt, ranks):
    return rank ^ jnp.where(chip == prompt, 0, 1) if ranks > 1 else rank


def merge_kernel(group, ranks, part_refs, out_refs, merged):
    count = out_refs[0].shape[0]
    dim = out_refs[0].shape[1] // group
    tops = [ref[:, dim + MAX_LANE : dim + MAX_LANE + 1] for ref in part_refs]
    top = functools.reduce(jnp.maximum, tops)
    total, summed = 0.0, 0.0
    for ref, part_top in zip(part_refs, tops):
        factor = jnp.exp(part_top - top)
        total = total + ref[:, dim + SUM_LANE : dim + SUM_LANE + 1] * factor
        summed = summed + ref[:, 0:dim] * factor
    merged[...] = summed / total
    me = lax.axis_index("seq")
    chip, rank = lax.div(me, ranks), lax.rem(me, ranks)
    prompt = lax.axis_index("prompt")
    for out_ref, side in zip(out_refs, (0, 1 if ranks > 1 else 0)):
        block = block_of(rank ^ side, chip, prompt, ranks)
        for g in range(group):
            place = pl.ds(block * (count * group) + g, count, stride=group)
            out_ref[:, g * dim : (g + 1) * dim] = merged[place, :].astype(BF16)


def project_kernel(ranks, head_refs, weight_refs, out_refs, all_heads):
    me = lax.axis_index("seq")
    chip, rank = lax.div(me, ranks), lax.rem(me, ranks)
    prompt = lax.axis_index("prompt")
    count = head_refs[0].shape[0]
    for x, ref in enumerate(head_refs):
        place = pl.multiple_of((chip ^ prompt ^ x) * count, count)
        all_heads[pl.ds(place, count), :] = ref[...].astype(F32)
    depth = weight_refs[0].shape[0]
    product = 0.0
    for y, ref in enumerate(weight_refs):
        columns = pl.ds(pl.multiple_of((rank ^ y) * depth, depth), depth)
        product = product + jnp.dot(
            all_heads[:, columns].astype(BF16), ref[...], preferred_element_type=F32
        )
    for x, ref in enumerate(out_refs):
        ref[...] = product[x * count : (x + 1) * count].astype(ref.dtype)


def call(kernel, out_shape, in_specs, scratch_shapes=(), aliases=None):
    return pl.pallas_call(
        kernel,
        out_shape=out_shape,
        in_specs=in_specs,
        out_specs=jax.tree.map(lambda _: pl.BlockSpec(memory_space=pltpu.VMEM), out_shape),
        scratch_shapes=scratch_shapes,
        input_output_aliases=aliases or {},
        compiler_params=pltpu.CompilerParams(vmem_limit_bytes=VMEM_LIMIT),
    )


def in_hbm(x):
    return pltpu.with_memory_space_constraint(x, pltpu.HBM)


def swap(x, axis, distance):
    return lax.ppermute(x, axis, [(i, i ^ distance) for i in range(lax.axis_size(axis))])


def joined(x, axis, combine):
    everything = jax.tree.map(lambda part: lax.all_gather(part, axis), x)
    initial = jax.tree.map(lambda part: part[0], everything)

    def lap(k, so_far):
        return combine(so_far, jax.tree.map(lambda part: part[k], everything))

    return lax.fori_loop(1, lax.axis_size(axis), lap, initial)


def combine(earlier, later):
    highest = jnp.maximum(earlier[0], later[0])
    early_factor = jnp.exp(earlier[0] - highest)
    late_factor = jnp.exp(later[0] - highest)
    softmax_total = earlier[1] * early_factor + later[1] * late_factor
    summed = earlier[2] * early_factor[..., None] + later[2] * late_factor[..., None]
    return (highest, softmax_total, summed)


def general_path(
    queries,
    prompt_key_cache,
    prompt_value_cache,
    kept,
    sample_keys,
    sample_values,
    suffix_len,
    decode_keys,
    decode_values,
    out_weight,
):
    seq_count = lax.axis_size("seq")
    seq_index = lax.axis_index("seq")
    own_count = queries.shape[1]
    step_count = queries.shape[2]
    head_count = queries.shape[3]
    head_dim = queries.shape[4]
    kv_count = prompt_key_cache.shape[1]
    group_size = head_count // kv_count
    logit_scale = 1.0 / math.sqrt(head_dim)
    gathered = lax.all_gather(queries, "seq", axis=1, tiled=True)
    sample_count = gathered.shape[1]
    grouped_queries = gathered[0].reshape(sample_count, step_count, kv_count, group_size, head_dim)
    query_rows = jnp.transpose(grouped_queries, (2, 0, 1, 3, 4)).reshape(
        kv_count, sample_count * step_count * group_size, head_dim
    )
    key_cache_store = prompt_key_cache[0].reshape(kv_count, KEPT_SLOTS, BLOCK_TOKENS, head_dim)
    value_cache_store = prompt_value_cache[0].reshape(kv_count, KEPT_SLOTS, BLOCK_TOKENS, head_dim)
    kept_block_counts = kept[0, :, 0]
    active_mask = jnp.arange(KEPT_SLOTS, dtype=jnp.int32)[None, :] < kept_block_counts[:, None]

    def one_head(pieces):
        head_row_block, key_block_list, value_block_list, live_blocks = pieces
        logit_scores = (
            jnp.einsum(
                "eg,mxg->emx", head_row_block, key_block_list, preferred_element_type=jnp.float32
            )
            * logit_scale
        )
        block_max = jnp.where(live_blocks[None, :], jnp.max(logit_scores, axis=2), NEGATIVE)
        attention_weights = jnp.where(
            live_blocks[None, :, None], jnp.exp(logit_scores - block_max[:, :, None]), 0.0
        )
        block_sum = jnp.sum(attention_weights, axis=2)
        block_output = jnp.einsum(
            "yaf,afi->yai",
            attention_weights.astype(jnp.bfloat16),
            value_block_list,
            preferred_element_type=jnp.float32,
        )
        highest = jnp.max(block_max, axis=1)
        factor = jnp.exp(block_max - highest[:, None])
        return (
            highest,
            jnp.sum(factor * block_sum, axis=1),
            jnp.sum(factor[:, :, None] * block_output, axis=1),
        )

    prompt_maximum, prompt_sum, prompt_output = lax.map(
        one_head, (query_rows, key_cache_store, value_cache_store, active_mask)
    )
    own_queries = queries[0].reshape(own_count, step_count, kv_count, group_size, head_dim)
    suffix_scores = (
        jnp.einsum(
            "nthgd,nhid->nhtgi", own_queries, sample_keys[0], preferred_element_type=jnp.float32
        )
        * logit_scale
    )
    fresh_scores = (
        jnp.einsum(
            "nthgd,nuhd->nhtgu", own_queries, decode_keys[0], preferred_element_type=jnp.float32
        )
        * logit_scale
    )
    position = jnp.arange(sample_keys.shape[3], dtype=jnp.int32)
    sample_token_mask = (position[None, :] < suffix_len[0][:, None])[:, None, None, None, :]
    step_index = jnp.arange(step_count, dtype=jnp.int32)
    newest_token_mask = (step_index[None, :] <= step_index[:, None])[None, None, :, None, :]
    tail_max = jnp.maximum(
        jnp.max(jnp.where(sample_token_mask, suffix_scores, NEGATIVE), axis=4),
        jnp.max(jnp.where(newest_token_mask, fresh_scores, NEGATIVE), axis=4),
    )
    suffix_weights = jnp.where(sample_token_mask, jnp.exp(suffix_scores - tail_max[..., None]), 0.0)
    fresh_weights = jnp.where(newest_token_mask, jnp.exp(fresh_scores - tail_max[..., None]), 0.0)
    tail_sum = jnp.sum(suffix_weights, axis=4) + jnp.sum(fresh_weights, axis=4)
    tail_out = jnp.einsum(
        "nhtgi,nhid->nhtgd",
        suffix_weights.astype(jnp.bfloat16),
        sample_values[0],
        preferred_element_type=jnp.float32,
    )
    tail_out = tail_out + jnp.einsum(
        "nhtgu,nuhd->nhtgd",
        fresh_weights.astype(jnp.bfloat16),
        decode_values[0],
        preferred_element_type=jnp.float32,
    )
    tail_part = (
        jnp.transpose(tail_max, (1, 0, 2, 3)),
        jnp.transpose(tail_sum, (1, 0, 2, 3)),
        jnp.transpose(tail_out, (1, 0, 2, 3, 4)),
    )
    prefix = (
        prompt_maximum.reshape(kv_count, sample_count, step_count, group_size),
        prompt_sum.reshape(kv_count, sample_count, step_count, group_size),
        prompt_output.reshape(kv_count, sample_count, step_count, group_size, head_dim),
    )
    offset = seq_index * own_count
    own_part = tuple((lax.dynamic_slice_in_dim(member, offset, own_count, 1) for member in prefix))
    merged = combine(own_part, tail_part)
    prefix = tuple(
        (
            lax.dynamic_update_slice_in_dim(member, update, offset, 1)
            for member, update in zip(prefix, merged)
        )
    )
    part_max = jnp.transpose(prefix[0], (1, 2, 0, 3)).reshape(sample_count, step_count, head_count)
    part_total = jnp.transpose(prefix[1], (1, 2, 0, 3)).reshape(
        sample_count, step_count, head_count
    )
    part_out = jnp.transpose(prefix[2], (1, 2, 0, 3, 4)).reshape(
        sample_count, step_count, head_count, head_dim
    )
    local_heads = head_count // seq_count
    highest, softmax_total, summed = joined((part_max, part_total, part_out), "seq", combine)
    highest = lax.dynamic_slice_in_dim(highest, seq_index * local_heads, local_heads, 2)
    softmax_total = lax.dynamic_slice_in_dim(softmax_total, seq_index * local_heads, local_heads, 2)
    summed = lax.dynamic_slice_in_dim(summed, seq_index * local_heads, local_heads, 2)
    head_out = (
        (summed / softmax_total[..., None])
        .astype(jnp.bfloat16)
        .reshape(sample_count * step_count, local_heads * head_dim)
    )
    all_rows = lax.all_gather(head_out, "prompt", axis=0, tiled=True)
    result = lax.psum_scatter(
        jnp.dot(all_rows, out_weight, preferred_element_type=jnp.float32),
        "seq",
        scatter_dimension=0,
        tiled=True,
    )
    return result.astype(jnp.bfloat16)


def cross(x, target):
    prompts, seqs = lax.axis_size("prompt"), lax.axis_size("seq")
    pairs = []
    for p in range(prompts):
        for s in range(seqs):
            to_p, to_s = target(p, s)
            pairs.append((p * seqs + s, to_p * seqs + to_s))
    return lax.ppermute(x, ("prompt", "seq"), pairs)


def on_device(
    queries,
    prompt_key_cache,
    prompt_value_cache,
    kept,
    sample_keys,
    sample_values,
    suffix_len,
    decode_keys,
    decode_values,
    out_weight,
):
    seq_count, prompt_count = lax.axis_size("seq"), lax.axis_size("prompt")
    if prompt_count != prompt_key_cache.shape[1]:
        return general_path(
            queries, prompt_key_cache, prompt_value_cache, kept, sample_keys, sample_values,
            suffix_len, decode_keys, decode_values, out_weight,
        )
    steps, head_count, dim = queries.shape[2:]
    heads, chunk = prompt_key_cache.shape[1:3]
    group = head_count // heads
    ranks = seq_count // heads
    shape = (heads, steps, group, dim, ranks, chunk)
    rows = steps * group
    vmem = pl.BlockSpec(memory_space=pltpu.VMEM)
    hbm = pl.BlockSpec(memory_space=pltpu.HBM)
    own_queries = queries.reshape(steps * head_count, dim)
    other_queries = [swap(own_queries, "seq", y) for y in range(1, ranks)]

    fetched = [
        own_queries,
        sample_keys[0, 0],
        sample_values[0, 0],
        decode_keys[0, 0],
        decode_values[0, 0],
        kept.reshape(heads),
        suffix_len.reshape(1),
    ]
    sources = [prompt_key_cache[0], prompt_value_cache[0], *fetched]
    message = jax.ShapeDtypeStruct((2 * chunk + (ranks + 3) * rows, dim), BF16)

    def run_message(*refs):
        n, m = len(sources), len(sources) + heads
        message_kernel(shape, refs[:n], refs[n:m], refs[m : m + len(fetched)], *refs[m + len(fetched) :])

    messages = call(
        run_message,
        [message] * heads,
        [hbm] * len(sources),
        [
            (pltpu.SMEM if x.dtype == jnp.int32 else pltpu.VMEM)(x.shape, x.dtype)
            for x in fetched
        ]
        + [
            pltpu.VMEM((heads, 4 * rows, dim), BF16),
            pltpu.SemaphoreType.DMA((len(fetched) + 2 * heads,)),
        ],
    )(*[x if x.size == 1 else in_hbm(x) for x in sources])

    def run_query(*refs):
        n = ranks - 1
        query_kernel(shape, refs[:n], refs[n + heads : n + 2 * heads], refs[-1])

    if ranks > 1:
        messages = call(
            run_query,
            [message] * heads,
            [vmem] * (ranks - 1 + heads),
            [pltpu.VMEM((heads, (ranks - 1) * rows, dim), BF16)],
            {ranks - 1 + x: x for x in range(heads)},
        )(*other_queries, *messages)
    late_weight, messages = lax.optimization_barrier((out_weight, messages))
    other_weights = [swap(late_weight, "seq", y) for y in range(1, ranks)]
    weight = call(
        fetch_kernel,
        jax.ShapeDtypeStruct(out_weight.shape, BF16),
        [pl.BlockSpec(memory_space=pl.ANY), hbm],
        [pltpu.SemaphoreType.DMA(())],
    )(messages[0], in_hbm(out_weight))
    messages = [messages[0]] + [swap(messages[x], "seq", x * ranks) for x in range(1, heads)]

    all_rows = seq_count * rows

    def run_prefix(*refs):
        prefix_kernel(shape, refs[:heads], *refs[heads:])

    part = call(
        run_prefix,
        jax.ShapeDtypeStruct((all_rows, 2 * dim), F32),
        [vmem] * heads,
        [pltpu.VMEM((all_rows, dim), BF16), pltpu.VMEM((all_rows, 2 * dim), F32)],
    )(*messages)
    parts = [part] + [swap(part, "seq", y) for y in range(1, ranks)]

    def run_merge(*refs):
        merge_kernel(group, ranks, refs[:ranks], refs[ranks : ranks + 2], refs[ranks + 2])

    count = all_rows // (ranks * group)
    staying, leaving = call(
        run_merge,
        [jax.ShapeDtypeStruct((count, group * dim), BF16)] * 2,
        [vmem] * ranks,
        [pltpu.VMEM((all_rows, dim), F32)],
    )(*parts)
    flip = 1 if ranks > 1 else 0
    head_outs = [staying] + [
        cross(leaving, lambda p, s, x=x: (p ^ x, s ^ flip)) for x in range(1, prompt_count)
    ]

    def run_project(*refs):
        n, m = prompt_count, prompt_count + ranks
        project_kernel(ranks, refs[:n], refs[n:m], refs[m : m + heads], refs[m + heads])

    terms = call(
        run_project,
        [
            jax.ShapeDtypeStruct((count, out_weight.shape[1]), BF16 if x else F32)
            for x in range(heads)
        ],
        [vmem] * (prompt_count + ranks),
        [pltpu.VMEM((prompt_count * count, group * dim), F32)],
    )(*head_outs, weight, *other_weights)
    result = terms[0]
    for x in reversed(range(1, heads)):
        result = result + swap(terms[x], "seq", x * ranks + flip).astype(F32)
    return result.astype(BF16)


def solution(mesh):
    placed = (
        P("prompt", "seq", None, None, None),
        P("prompt", None, "seq", None),
        P("prompt", None, "seq", None),
        P("prompt", None, "seq"),
        P("prompt", "seq", None, None, None),
        P("prompt", "seq", None, None, None),
        P("prompt", "seq"),
        P("prompt", "seq", None, None, None),
        P("prompt", "seq", None, None, None),
        P("seq", "prompt"),
    )
    return jax.shard_map(
        on_device, mesh=mesh, in_specs=placed, out_specs=P("seq", "prompt"), check_vma=False
    )
```

```python
import functools
import math

import jax
import jax.numpy as jnp
from jax import lax
from jax.experimental import pallas as pl
from jax.experimental.pallas import tpu as pltpu
from jax.sharding import PartitionSpec as P

BLOCK_TOKENS = 128
KEPT_SLOTS = 2
NEGATIVE = -1e30
F32 = jnp.float32
BF16 = jnp.bfloat16
VMEM_LIMIT = 16 * 1024 * 1024
MAX_LANE, SUM_LANE = 0, 1


def lanes_of(rows, width, values):
    lane = lax.broadcasted_iota(jnp.int32, (rows, width), 1)
    filled = jnp.zeros((rows, width), F32)
    for i, value in enumerate(values):
        filled = jnp.where(lane == i, jnp.asarray(value, F32), filled)
    return filled


def in_pieces(x, count):
    pieces = []
    for _ in range(count):
        pieces.append(x.astype(BF16))
        x = x - pieces[-1].astype(F32)
    return pieces


def dot_rows(a, b):
    return lax.dot_general(a, b, (((1,), (1,)), ((), ())), preferred_element_type=F32)


def copy_all(pairs, sems):
    copies = [
        pltpu.make_async_copy(source, target, sems.at[i]) for i, (source, target) in enumerate(pairs)
    ]
    for copy in copies:
        copy.start()
    return copies


def message_kernel(shape, in_refs, out_refs, held, small, sems):
    heads, steps, group, dim, ranks, chunk = shape
    rows = steps * group
    scale = 1.0 / math.sqrt(dim)
    chip = lax.div(lax.axis_index("seq"), ranks)
    key_ref, value_ref, *fetched = in_refs
    pairs = list(zip(fetched, held))
    for x in range(heads):
        pairs.append((key_ref.at[chip ^ x], out_refs[x].at[0:chunk]))
        pairs.append((value_ref.at[chip ^ x], out_refs[x].at[chunk : 2 * chunk]))
    copies = [
        pltpu.make_async_copy(source, target, sems.at[i]) for i, (source, target) in enumerate(pairs)
    ]
    for copy in copies:
        copy.start()
    for copy in copies[: len(held)]:
        copy.wait()
    q_ref, tail_key_ref, tail_value_ref, step_key_ref, step_value_ref, kept_ref, len_ref = held
    queries = q_ref[...].astype(F32)
    step_keys = step_key_ref[...].astype(F32)
    step_values = step_value_ref[...].astype(F32)
    all_rows = heads * rows
    q = jnp.concatenate([rows_of_head(queries, shape, h) for h in range(heads)], axis=0)
    q_narrow = q.astype(BF16)

    def by_head(x):
        return [x[h * rows : (h + 1) * rows] for h in range(heads)]

    def spread(x):
        return jnp.concatenate([jnp.broadcast_to(x[h : h + 1], (rows, dim)) for h in range(heads)], axis=0)

    scores = jnp.concatenate(
        [dot_rows(part, tail_key_ref[h]) for h, part in enumerate(by_head(q_narrow))], axis=0
    )
    position = lax.broadcasted_iota(jnp.int32, scores.shape, 1)
    scores = jnp.where(position < len_ref[0], scores * scale, NEGATIVE)
    row = lax.broadcasted_iota(jnp.int32, (all_rows, 1), 0)
    step_of_row = lax.rem(lax.div(row, group), steps)
    own = []
    for u in range(steps):
        score = jnp.sum(q * spread(step_keys[u]), axis=1, keepdims=True) * scale
        own.append(jnp.where(step_of_row >= u, score, NEGATIVE))
    top = functools.reduce(jnp.maximum, own, jnp.max(scores, axis=1, keepdims=True))
    weights = jnp.exp(scores - top)
    total = jnp.sum(weights, axis=1, keepdims=True)
    summed = jnp.concatenate(
        [
            jnp.dot(part, tail_value_ref[h], preferred_element_type=F32)
            for h, part in enumerate(by_head(weights.astype(BF16)))
        ],
        axis=0,
    )
    for u, score in enumerate(own):
        weight = jnp.exp(score - top)
        total = total + weight
        summed = summed + weight.astype(BF16).astype(F32) * spread(step_values[u])
    summed_high, summed_rest = in_pieces(summed, 2)
    kept = jnp.concatenate([jnp.full((rows, 1), kept_ref[h].astype(F32)) for h in range(heads)], axis=0)
    stats = lanes_of(all_rows, dim, [*in_pieces(top, 3), *in_pieces(total, 3), kept]).astype(BF16)
    for i, part in enumerate([summed_high, summed_rest, stats, q_narrow]):
        for h, piece in enumerate(by_head(part)):
            small[h, i * rows : (i + 1) * rows, :] = piece
    for x in range(heads):
        out_refs[x][2 * chunk : 2 * chunk + 4 * rows, :] = small[chip ^ x]
    for copy in copies[len(held) :]:
        copy.wait()


def rows_of_head(whole, shape, h):
    heads, steps, group, *_ = shape
    return jnp.concatenate(
        [
            whole[(t * heads + h) * group : (t * heads + h + 1) * group]
            for t in range(steps)
        ],
        axis=0,
    )


def query_kernel(shape, q_refs, out_refs, small):
    heads, steps, group, dim, ranks, chunk = shape
    rows = steps * group
    chip = lax.div(lax.axis_index("seq"), ranks)
    for y, ref in enumerate(q_refs):
        queries = ref[...].astype(F32)
        for h in range(heads):
            small[h, y * rows : (y + 1) * rows, :] = rows_of_head(queries, shape, h).astype(BF16)
    start = 2 * chunk + 4 * rows
    for x in range(heads):
        out_refs[x][start : start + len(q_refs) * rows, :] = small[chip ^ x]


def fetch_kernel(after_ref, weight_ref, out_ref, sem):
    copy = pltpu.make_async_copy(weight_ref, out_ref, sem)
    copy.start()
    copy.wait()


def prefix_kernel(shape, message_refs, out_ref, q_all, tails):
    heads, steps, group, dim, ranks, chunk = shape
    rows = steps * group
    scale = 1.0 / math.sqrt(dim)
    me = lax.axis_index("seq")
    chip, rank = lax.div(me, ranks), lax.rem(me, ranks)
    all_rows = q_all.shape[0]
    tails[:, 0:dim] = jnp.zeros((all_rows, dim), F32)
    tails[:, dim:] = lanes_of(all_rows, dim, [NEGATIVE])
    kept = []
    for x in range(heads):
        base = (chip ^ x) * ranks
        start = 2 * chunk
        place = pl.multiple_of((base + rank) * rows, rows)
        high = message_refs[x][start : start + rows, :].astype(F32)
        rest = message_refs[x][start + rows : start + 2 * rows, :].astype(F32)
        stats = message_refs[x][start + 2 * rows : start + 3 * rows, :].astype(F32)
        start += 3 * rows
        for y in range(ranks):
            row = pl.multiple_of((base + (rank ^ y)) * rows, rows)
            q_all[pl.ds(row, rows), :] = message_refs[x][start + y * rows : start + (y + 1) * rows, :]
        tails[pl.ds(place, rows), 0:dim] = high + rest
        tail_top = stats[:, 0:1] + stats[:, 1:2] + stats[:, 2:3]
        total = stats[:, 3:4] + stats[:, 4:5] + stats[:, 5:6]
        tails[pl.ds(place, rows), dim:] = lanes_of(rows, dim, [tail_top, total])
        kept.append(stats[0:1, 6:7])
    block = lax.div(lax.broadcasted_iota(jnp.int32, (1, chunk), 1), BLOCK_TOKENS).astype(F32)
    q = q_all[...]
    tail_top = tails[:, dim + MAX_LANE : dim + MAX_LANE + 1]
    top = tail_top
    scores = []
    for x in range(heads):
        score = dot_rows(q, message_refs[x][0:chunk, :]) * scale
        score = jnp.where(block < kept[x], score, NEGATIVE)
        top = jnp.maximum(top, jnp.max(score, axis=1, keepdims=True))
        scores.append(score)
    factor = jnp.exp(tail_top - top)
    total = tails[:, dim + SUM_LANE : dim + SUM_LANE + 1] * factor
    summed = tails[:, 0:dim] * factor
    for x in range(heads):
        weights = jnp.exp(scores[x] - top)
        total = total + jnp.sum(weights, axis=1, keepdims=True)
        summed = summed + jnp.dot(
            weights.astype(BF16),
            message_refs[x][chunk : 2 * chunk, :],
            preferred_element_type=F32,
        )
    out_ref[:, 0:dim] = summed
    out_ref[:, dim:] = lanes_of(all_rows, dim, [top, total])


def block_of(rank, chip, prompt, ranks):
    return rank ^ jnp.where(chip == prompt, 0, 1) if ranks > 1 else rank


def merge_kernel(group, ranks, part_refs, out_refs, merged):
    count = out_refs[0].shape[0]
    dim = out_refs[0].shape[1] // group
    tops = [ref[:, dim + MAX_LANE : dim + MAX_LANE + 1] for ref in part_refs]
    top = functools.reduce(jnp.maximum, tops)
    total, summed = 0.0, 0.0
    for ref, part_top in zip(part_refs, tops):
        factor = jnp.exp(part_top - top)
        total = total + ref[:, dim + SUM_LANE : dim + SUM_LANE + 1] * factor
        summed = summed + ref[:, 0:dim] * factor
    merged[...] = summed / total
    me = lax.axis_index("seq")
    chip, rank = lax.div(me, ranks), lax.rem(me, ranks)
    prompt = lax.axis_index("prompt")
    for out_ref, side in zip(out_refs, (0, 1 if ranks > 1 else 0)):
        block = block_of(rank ^ side, chip, prompt, ranks)
        for g in range(group):
            place = pl.ds(block * (count * group) + g, count, stride=group)
            out_ref[:, g * dim : (g + 1) * dim] = merged[place, :].astype(BF16)


def project_kernel(ranks, head_refs, weight_refs, out_refs, all_heads):
    me = lax.axis_index("seq")
    chip, rank = lax.div(me, ranks), lax.rem(me, ranks)
    prompt = lax.axis_index("prompt")
    count = head_refs[0].shape[0]
    for x, ref in enumerate(head_refs):
        place = pl.multiple_of((chip ^ prompt ^ x) * count, count)
        all_heads[pl.ds(place, count), :] = ref[...].astype(F32)
    depth = weight_refs[0].shape[0]
    product = 0.0
    for y, ref in enumerate(weight_refs):
        columns = pl.ds(pl.multiple_of((rank ^ y) * depth, depth), depth)
        product = product + jnp.dot(
            all_heads[:, columns].astype(BF16), ref[...], preferred_element_type=F32
        )
    for x, ref in enumerate(out_refs):
        ref[...] = product[x * count : (x + 1) * count].astype(ref.dtype)


def call(kernel, out_shape, in_specs, scratch_shapes=(), aliases=None):
    return pl.pallas_call(
        kernel,
        out_shape=out_shape,
        in_specs=in_specs,
        out_specs=jax.tree.map(lambda _: pl.BlockSpec(memory_space=pltpu.VMEM), out_shape),
        scratch_shapes=scratch_shapes,
        input_output_aliases=aliases or {},
        compiler_params=pltpu.CompilerParams(vmem_limit_bytes=VMEM_LIMIT),
    )


def in_hbm(x):
    return pltpu.with_memory_space_constraint(x, pltpu.HBM)


def swap(x, axis, distance):
    return lax.ppermute(x, axis, [(i, i ^ distance) for i in range(lax.axis_size(axis))])


def joined(x, axis, combine):
    everything = jax.tree.map(lambda part: lax.all_gather(part, axis), x)
    initial = jax.tree.map(lambda part: part[0], everything)

    def lap(k, so_far):
        return combine(so_far, jax.tree.map(lambda part: part[k], everything))

    return lax.fori_loop(1, lax.axis_size(axis), lap, initial)


def combine(earlier, later):
    highest = jnp.maximum(earlier[0], later[0])
    early_factor = jnp.exp(earlier[0] - highest)
    late_factor = jnp.exp(later[0] - highest)
    softmax_total = earlier[1] * early_factor + later[1] * late_factor
    summed = earlier[2] * early_factor[..., None] + later[2] * late_factor[..., None]
    return (highest, softmax_total, summed)


def general_path(
    queries,
    prompt_key_cache,
    prompt_value_cache,
    kept,
    sample_keys,
    sample_values,
    suffix_len,
    decode_keys,
    decode_values,
    out_weight,
):
    seq_count = lax.axis_size("seq")
    seq_index = lax.axis_index("seq")
    own_count = queries.shape[1]
    step_count = queries.shape[2]
    head_count = queries.shape[3]
    head_dim = queries.shape[4]
    kv_count = prompt_key_cache.shape[1]
    group_size = head_count // kv_count
    logit_scale = 1.0 / math.sqrt(head_dim)
    gathered = lax.all_gather(queries, "seq", axis=1, tiled=True)
    sample_count = gathered.shape[1]
    grouped_queries = gathered[0].reshape(sample_count, step_count, kv_count, group_size, head_dim)
    query_rows = jnp.transpose(grouped_queries, (2, 0, 1, 3, 4)).reshape(
        kv_count, sample_count * step_count * group_size, head_dim
    )
    key_cache_store = prompt_key_cache[0].reshape(kv_count, KEPT_SLOTS, BLOCK_TOKENS, head_dim)
    value_cache_store = prompt_value_cache[0].reshape(kv_count, KEPT_SLOTS, BLOCK_TOKENS, head_dim)
    kept_block_counts = kept[0, :, 0]
    active_mask = jnp.arange(KEPT_SLOTS, dtype=jnp.int32)[None, :] < kept_block_counts[:, None]

    def one_head(pieces):
        head_row_block, key_block_list, value_block_list, live_blocks = pieces
        logit_scores = (
            jnp.einsum(
                "eg,mxg->emx", head_row_block, key_block_list, preferred_element_type=jnp.float32
            )
            * logit_scale
        )
        block_max = jnp.where(live_blocks[None, :], jnp.max(logit_scores, axis=2), NEGATIVE)
        attention_weights = jnp.where(
            live_blocks[None, :, None], jnp.exp(logit_scores - block_max[:, :, None]), 0.0
        )
        block_sum = jnp.sum(attention_weights, axis=2)
        block_output = jnp.einsum(
            "yaf,afi->yai",
            attention_weights.astype(jnp.bfloat16),
            value_block_list,
            preferred_element_type=jnp.float32,
        )
        highest = jnp.max(block_max, axis=1)
        factor = jnp.exp(block_max - highest[:, None])
        return (
            highest,
            jnp.sum(factor * block_sum, axis=1),
            jnp.sum(factor[:, :, None] * block_output, axis=1),
        )

    prompt_maximum, prompt_sum, prompt_output = lax.map(
        one_head, (query_rows, key_cache_store, value_cache_store, active_mask)
    )
    own_queries = queries[0].reshape(own_count, step_count, kv_count, group_size, head_dim)
    suffix_scores = (
        jnp.einsum(
            "nthgd,nhid->nhtgi", own_queries, sample_keys[0], preferred_element_type=jnp.float32
        )
        * logit_scale
    )
    fresh_scores = (
        jnp.einsum(
            "nthgd,nuhd->nhtgu", own_queries, decode_keys[0], preferred_element_type=jnp.float32
        )
        * logit_scale
    )
    position = jnp.arange(sample_keys.shape[3], dtype=jnp.int32)
    sample_token_mask = (position[None, :] < suffix_len[0][:, None])[:, None, None, None, :]
    step_index = jnp.arange(step_count, dtype=jnp.int32)
    newest_token_mask = (step_index[None, :] <= step_index[:, None])[None, None, :, None, :]
    tail_max = jnp.maximum(
        jnp.max(jnp.where(sample_token_mask, suffix_scores, NEGATIVE), axis=4),
        jnp.max(jnp.where(newest_token_mask, fresh_scores, NEGATIVE), axis=4),
    )
    suffix_weights = jnp.where(sample_token_mask, jnp.exp(suffix_scores - tail_max[..., None]), 0.0)
    fresh_weights = jnp.where(newest_token_mask, jnp.exp(fresh_scores - tail_max[..., None]), 0.0)
    tail_sum = jnp.sum(suffix_weights, axis=4) + jnp.sum(fresh_weights, axis=4)
    tail_out = jnp.einsum(
        "nhtgi,nhid->nhtgd",
        suffix_weights.astype(jnp.bfloat16),
        sample_values[0],
        preferred_element_type=jnp.float32,
    )
    tail_out = tail_out + jnp.einsum(
        "nhtgu,nuhd->nhtgd",
        fresh_weights.astype(jnp.bfloat16),
        decode_values[0],
        preferred_element_type=jnp.float32,
    )
    tail_part = (
        jnp.transpose(tail_max, (1, 0, 2, 3)),
        jnp.transpose(tail_sum, (1, 0, 2, 3)),
        jnp.transpose(tail_out, (1, 0, 2, 3, 4)),
    )
    prefix = (
        prompt_maximum.reshape(kv_count, sample_count, step_count, group_size),
        prompt_sum.reshape(kv_count, sample_count, step_count, group_size),
        prompt_output.reshape(kv_count, sample_count, step_count, group_size, head_dim),
    )
    offset = seq_index * own_count
    own_part = tuple((lax.dynamic_slice_in_dim(member, offset, own_count, 1) for member in prefix))
    merged = combine(own_part, tail_part)
    prefix = tuple(
        (
            lax.dynamic_update_slice_in_dim(member, update, offset, 1)
            for member, update in zip(prefix, merged)
        )
    )
    part_max = jnp.transpose(prefix[0], (1, 2, 0, 3)).reshape(sample_count, step_count, head_count)
    part_total = jnp.transpose(prefix[1], (1, 2, 0, 3)).reshape(
        sample_count, step_count, head_count
    )
    part_out = jnp.transpose(prefix[2], (1, 2, 0, 3, 4)).reshape(
        sample_count, step_count, head_count, head_dim
    )
    local_heads = head_count // seq_count
    highest, softmax_total, summed = joined((part_max, part_total, part_out), "seq", combine)
    highest = lax.dynamic_slice_in_dim(highest, seq_index * local_heads, local_heads, 2)
    softmax_total = lax.dynamic_slice_in_dim(softmax_total, seq_index * local_heads, local_heads, 2)
    summed = lax.dynamic_slice_in_dim(summed, seq_index * local_heads, local_heads, 2)
    head_out = (
        (summed / softmax_total[..., None])
        .astype(jnp.bfloat16)
        .reshape(sample_count * step_count, local_heads * head_dim)
    )
    all_rows = lax.all_gather(head_out, "prompt", axis=0, tiled=True)
    result = lax.psum_scatter(
        jnp.dot(all_rows, out_weight, preferred_element_type=jnp.float32),
        "seq",
        scatter_dimension=0,
        tiled=True,
    )
    return result.astype(jnp.bfloat16)


def cross(x, target):
    prompts, seqs = lax.axis_size("prompt"), lax.axis_size("seq")
    pairs = []
    for p in range(prompts):
        for s in range(seqs):
            to_p, to_s = target(p, s)
            pairs.append((p * seqs + s, to_p * seqs + to_s))
    return lax.ppermute(x, ("prompt", "seq"), pairs)


def on_device(
    queries,
    prompt_key_cache,
    prompt_value_cache,
    kept,
    sample_keys,
    sample_values,
    suffix_len,
    decode_keys,
    decode_values,
    out_weight,
):
    seq_count, prompt_count = lax.axis_size("seq"), lax.axis_size("prompt")
    if prompt_count != prompt_key_cache.shape[1]:
        return general_path(
            queries, prompt_key_cache, prompt_value_cache, kept, sample_keys, sample_values,
            suffix_len, decode_keys, decode_values, out_weight,
        )
    steps, head_count, dim = queries.shape[2:]
    heads, chunk = prompt_key_cache.shape[1:3]
    group = head_count // heads
    ranks = seq_count // heads
    shape = (heads, steps, group, dim, ranks, chunk)
    rows = steps * group
    vmem = pl.BlockSpec(memory_space=pltpu.VMEM)
    hbm = pl.BlockSpec(memory_space=pltpu.HBM)
    own_queries = queries.reshape(steps * head_count, dim)
    other_queries = [swap(own_queries, "seq", y) for y in range(1, ranks)]

    fetched = [
        own_queries,
        sample_keys[0, 0],
        sample_values[0, 0],
        decode_keys[0, 0],
        decode_values[0, 0],
        kept.reshape(heads),
        suffix_len.reshape(1),
    ]
    sources = [prompt_key_cache[0], prompt_value_cache[0], *fetched]
    message = jax.ShapeDtypeStruct((2 * chunk + (ranks + 3) * rows, dim), BF16)

    def run_message(*refs):
        n, m = len(sources), len(sources) + heads
        message_kernel(shape, refs[:n], refs[n:m], refs[m : m + len(fetched)], *refs[m + len(fetched) :])

    messages = call(
        run_message,
        [message] * heads,
        [hbm] * len(sources),
        [
            (pltpu.SMEM if x.dtype == jnp.int32 else pltpu.VMEM)(x.shape, x.dtype)
            for x in fetched
        ]
        + [
            pltpu.VMEM((heads, 4 * rows, dim), BF16),
            pltpu.SemaphoreType.DMA((len(fetched) + 2 * heads,)),
        ],
    )(*[x if x.size == 1 else in_hbm(x) for x in sources])

    def run_query(*refs):
        n = ranks - 1
        query_kernel(shape, refs[:n], refs[n + heads : n + 2 * heads], refs[-1])

    if ranks > 1:
        messages = call(
            run_query,
            [message] * heads,
            [vmem] * (ranks - 1 + heads),
            [pltpu.VMEM((heads, (ranks - 1) * rows, dim), BF16)],
            {ranks - 1 + x: x for x in range(heads)},
        )(*other_queries, *messages)
    late_weight, messages = lax.optimization_barrier((out_weight, messages))
    other_weights = [swap(late_weight, "seq", y) for y in range(1, ranks)]
    weight = call(
        fetch_kernel,
        jax.ShapeDtypeStruct(out_weight.shape, BF16),
        [pl.BlockSpec(memory_space=pl.ANY), hbm],
        [pltpu.SemaphoreType.DMA(())],
    )(messages[0], in_hbm(out_weight))
    messages = [messages[0]] + [swap(messages[x], "seq", x * ranks) for x in range(1, heads)]

    all_rows = seq_count * rows

    def run_prefix(*refs):
        prefix_kernel(shape, refs[:heads], *refs[heads + 1 :])

    part = call(
        run_prefix,
        jax.ShapeDtypeStruct((all_rows, 2 * dim), F32),
        [vmem] * heads + [pl.BlockSpec(memory_space=pl.ANY)],
        [pltpu.VMEM((all_rows, dim), BF16), pltpu.VMEM((all_rows, 2 * dim), F32)],
    )(*messages, weight)
    parts = [part] + [swap(part, "seq", y) for y in range(1, ranks)]

    def run_merge(*refs):
        merge_kernel(group, ranks, refs[:ranks], refs[ranks : ranks + 2], refs[ranks + 2])

    count = all_rows // (ranks * group)
    staying, leaving = call(
        run_merge,
        [jax.ShapeDtypeStruct((count, group * dim), BF16)] * 2,
        [vmem] * ranks,
        [pltpu.VMEM((all_rows, dim), F32)],
    )(*parts)
    flip = 1 if ranks > 1 else 0
    head_outs = [staying] + [
        cross(leaving, lambda p, s, x=x: (p ^ x, s ^ flip)) for x in range(1, prompt_count)
    ]

    def run_project(*refs):
        n, m = prompt_count, prompt_count + ranks
        project_kernel(ranks, refs[:n], refs[n:m], refs[m : m + heads], refs[m + heads])

    terms = call(
        run_project,
        [
            jax.ShapeDtypeStruct((count, out_weight.shape[1]), BF16 if x else F32)
            for x in range(heads)
        ],
        [vmem] * (prompt_count + ranks),
        [pltpu.VMEM((prompt_count * count, group * dim), F32)],
    )(*head_outs, weight, *other_weights)
    result = terms[0]
    for x in reversed(range(1, heads)):
        result = result + swap(terms[x], "seq", x * ranks + flip).astype(F32)
    return result.astype(BF16)


def solution(mesh):
    placed = (
        P("prompt", "seq", None, None, None),
        P("prompt", None, "seq", None),
        P("prompt", None, "seq", None),
        P("prompt", None, "seq"),
        P("prompt", "seq", None, None, None),
        P("prompt", "seq", None, None, None),
        P("prompt", "seq"),
        P("prompt", "seq", None, None, None),
        P("prompt", "seq", None, None, None),
        P("seq", "prompt"),
    )
    return jax.shard_map(
        on_device, mesh=mesh, in_specs=placed, out_specs=P("seq", "prompt"), check_vma=False
    )
```

```python
import functools
import math

import jax
import jax.numpy as jnp
from jax import lax
from jax.experimental import pallas as pl
from jax.experimental.pallas import tpu as pltpu
from jax.sharding import PartitionSpec as P

BLOCK_TOKENS = 128
KEPT_SLOTS = 2
NEGATIVE = -1e30
F32 = jnp.float32
BF16 = jnp.bfloat16
VMEM_LIMIT = 16 * 1024 * 1024
MAX_LANE, SUM_LANE = 0, 1


def lanes_of(rows, width, values):
    lane = lax.broadcasted_iota(jnp.int32, (rows, width), 1)
    filled = jnp.zeros((rows, width), F32)
    for i, value in enumerate(values):
        filled = jnp.where(lane == i, jnp.asarray(value, F32), filled)
    return filled


def in_pieces(x, count):
    pieces = []
    for _ in range(count):
        pieces.append(x.astype(BF16))
        x = x - pieces[-1].astype(F32)
    return pieces


def dot_rows(a, b):
    return lax.dot_general(a, b, (((1,), (1,)), ((), ())), preferred_element_type=F32)


def copy_all(pairs, sems):
    copies = [
        pltpu.make_async_copy(source, target, sems.at[i]) for i, (source, target) in enumerate(pairs)
    ]
    for copy in copies:
        copy.start()
    return copies


def message_kernel(shape, in_refs, out_refs, held, small, sems):
    heads, steps, group, dim, ranks, chunk = shape
    rows = steps * group
    scale = 1.0 / math.sqrt(dim)
    chip = lax.div(lax.axis_index("seq"), ranks)
    key_ref, value_ref, *fetched = in_refs
    pairs = list(zip(fetched, held))
    for x in range(heads):
        pairs.append((key_ref.at[chip ^ x], out_refs[x].at[0:chunk]))
        pairs.append((value_ref.at[chip ^ x], out_refs[x].at[chunk : 2 * chunk]))
    copies = [
        pltpu.make_async_copy(source, target, sems.at[i]) for i, (source, target) in enumerate(pairs)
    ]
    for copy in copies:
        copy.start()
    for copy in copies[: len(held)]:
        copy.wait()
    q_ref, tail_key_ref, tail_value_ref, step_key_ref, step_value_ref, kept_ref, len_ref = held
    queries = q_ref[...].astype(F32)
    step_keys = step_key_ref[...].astype(F32)
    step_values = step_value_ref[...].astype(F32)
    all_rows = heads * rows
    q = jnp.concatenate([rows_of_head(queries, shape, h) for h in range(heads)], axis=0)
    q_narrow = q.astype(BF16)

    def by_head(x):
        return [x[h * rows : (h + 1) * rows] for h in range(heads)]

    def spread(x):
        return jnp.concatenate([jnp.broadcast_to(x[h : h + 1], (rows, dim)) for h in range(heads)], axis=0)

    scores = jnp.concatenate(
        [dot_rows(part, tail_key_ref[h]) for h, part in enumerate(by_head(q_narrow))], axis=0
    )
    position = lax.broadcasted_iota(jnp.int32, scores.shape, 1)
    scores = jnp.where(position < len_ref[0], scores * scale, NEGATIVE)
    row = lax.broadcasted_iota(jnp.int32, (all_rows, 1), 0)
    step_of_row = lax.rem(lax.div(row, group), steps)
    own = []
    for u in range(steps):
        score = jnp.sum(q * spread(step_keys[u]), axis=1, keepdims=True) * scale
        own.append(jnp.where(step_of_row >= u, score, NEGATIVE))
    top = functools.reduce(jnp.maximum, own, jnp.max(scores, axis=1, keepdims=True))
    weights = jnp.exp(scores - top)
    total = jnp.sum(weights, axis=1, keepdims=True)
    summed = jnp.concatenate(
        [
            jnp.dot(part, tail_value_ref[h], preferred_element_type=F32)
            for h, part in enumerate(by_head(weights.astype(BF16)))
        ],
        axis=0,
    )
    for u, score in enumerate(own):
        weight = jnp.exp(score - top)
        total = total + weight
        summed = summed + weight.astype(BF16).astype(F32) * spread(step_values[u])
    summed_high, summed_rest = in_pieces(summed, 2)
    kept = jnp.concatenate([jnp.full((rows, 1), kept_ref[h].astype(F32)) for h in range(heads)], axis=0)
    stats = lanes_of(all_rows, dim, [*in_pieces(top, 3), *in_pieces(total, 3), kept]).astype(BF16)
    for i, part in enumerate([summed_high, summed_rest, stats, q_narrow]):
        for h, piece in enumerate(by_head(part)):
            small[h, i * rows : (i + 1) * rows, :] = piece
    for x in range(heads):
        out_refs[x][2 * chunk : 2 * chunk + 4 * rows, :] = small[chip ^ x]
    for copy in copies[len(held) :]:
        copy.wait()


def rows_of_head(whole, shape, h):
    heads, steps, group, *_ = shape
    return jnp.concatenate(
        [
            whole[(t * heads + h) * group : (t * heads + h + 1) * group]
            for t in range(steps)
        ],
        axis=0,
    )


def query_kernel(shape, q_refs, out_refs, small):
    heads, steps, group, dim, ranks, chunk = shape
    rows = steps * group
    chip = lax.div(lax.axis_index("seq"), ranks)
    for y, ref in enumerate(q_refs):
        queries = ref[...].astype(F32)
        for h in range(heads):
            small[h, y * rows : (y + 1) * rows, :] = rows_of_head(queries, shape, h).astype(BF16)
    start = 2 * chunk + 4 * rows
    for x in range(heads):
        out_refs[x][start : start + len(q_refs) * rows, :] = small[chip ^ x]


def fetch_kernel(after_ref, weight_ref, out_ref, sem):
    copy = pltpu.make_async_copy(weight_ref, out_ref, sem)
    copy.start()
    copy.wait()


def prefix_kernel(shape, message_refs, out_ref, q_all, tails):
    heads, steps, group, dim, ranks, chunk = shape
    rows = steps * group
    scale = 1.0 / math.sqrt(dim)
    me = lax.axis_index("seq")
    chip, rank = lax.div(me, ranks), lax.rem(me, ranks)
    all_rows = q_all.shape[0]
    tails[:, 0:dim] = jnp.zeros((all_rows, dim), F32)
    tails[:, dim:] = lanes_of(all_rows, dim, [NEGATIVE])
    kept = []
    for x in range(heads):
        base = (chip ^ x) * ranks
        start = 2 * chunk
        place = pl.multiple_of((base + rank) * rows, rows)
        high = message_refs[x][start : start + rows, :].astype(F32)
        rest = message_refs[x][start + rows : start + 2 * rows, :].astype(F32)
        stats = message_refs[x][start + 2 * rows : start + 3 * rows, :].astype(F32)
        start += 3 * rows
        for y in range(ranks):
            row = pl.multiple_of((base + (rank ^ y)) * rows, rows)
            q_all[pl.ds(row, rows), :] = message_refs[x][start + y * rows : start + (y + 1) * rows, :]
        tails[pl.ds(place, rows), 0:dim] = high + rest
        tail_top = stats[:, 0:1] + stats[:, 1:2] + stats[:, 2:3]
        total = stats[:, 3:4] + stats[:, 4:5] + stats[:, 5:6]
        tails[pl.ds(place, rows), dim:] = lanes_of(rows, dim, [tail_top, total])
        kept.append(stats[0:1, 6:7])
    block = lax.div(lax.broadcasted_iota(jnp.int32, (1, chunk), 1), BLOCK_TOKENS).astype(F32)
    q = q_all[...]
    tail_top = tails[:, dim + MAX_LANE : dim + MAX_LANE + 1]
    top = tail_top
    scores = []
    for x in range(heads):
        score = dot_rows(q, message_refs[x][0:chunk, :]) * scale
        score = jnp.where(block < kept[x], score, NEGATIVE)
        top = jnp.maximum(top, jnp.max(score, axis=1, keepdims=True))
        scores.append(score)
    factor = jnp.exp(tail_top - top)
    total = tails[:, dim + SUM_LANE : dim + SUM_LANE + 1] * factor
    summed = tails[:, 0:dim] * factor
    for x in range(heads):
        weights = jnp.exp(scores[x] - top)
        total = total + jnp.sum(weights, axis=1, keepdims=True)
        summed = summed + jnp.dot(
            weights.astype(BF16),
            message_refs[x][chunk : 2 * chunk, :],
            preferred_element_type=F32,
        )
    out_ref[:, 0:dim] = summed
    out_ref[:, dim:] = lanes_of(all_rows, dim, [top, total])


def block_of(rank, chip, prompt, ranks):
    return rank ^ jnp.where(chip == prompt, 0, 1) if ranks > 1 else rank


def merge_kernel(group, ranks, part_refs, out_refs, merged):
    count = out_refs[0].shape[0]
    dim = out_refs[0].shape[1] // group
    tops = [ref[:, dim + MAX_LANE : dim + MAX_LANE + 1] for ref in part_refs]
    top = functools.reduce(jnp.maximum, tops)
    total, summed = 0.0, 0.0
    for ref, part_top in zip(part_refs, tops):
        factor = jnp.exp(part_top - top)
        total = total + ref[:, dim + SUM_LANE : dim + SUM_LANE + 1] * factor
        summed = summed + ref[:, 0:dim] * factor
    merged[...] = summed / total
    me = lax.axis_index("seq")
    chip, rank = lax.div(me, ranks), lax.rem(me, ranks)
    prompt = lax.axis_index("prompt")
    for out_ref, side in zip(out_refs, (0, 1 if ranks > 1 else 0)):
        block = block_of(rank ^ side, chip, prompt, ranks)
        for g in range(group):
            place = pl.ds(block * (count * group) + g, count, stride=group)
            out_ref[:, g * dim : (g + 1) * dim] = merged[place, :].astype(BF16)


def prompt_targets(count):
    if count == 4:
        return ((1, 0, 3, 2), (3, 2, 0, 1), (2, 3, 1, 0))
    return tuple(tuple(p ^ x for p in range(count)) for x in range(1, count))


def project_kernel(ranks, head_refs, weight_refs, out_refs, all_heads):
    me = lax.axis_index("seq")
    chip, rank = lax.div(me, ranks), lax.rem(me, ranks)
    prompt = lax.axis_index("prompt")
    count = head_refs[0].shape[0]
    for x, ref in enumerate(head_refs):
        sender = prompt
        if x:
            for p, target in enumerate(prompt_targets(len(head_refs))[x - 1]):
                sender = jnp.where(prompt == target, p, sender)
        place = pl.multiple_of((chip ^ sender) * count, count)
        all_heads[pl.ds(place, count), :] = ref[...].astype(F32)
    depth = weight_refs[0].shape[0]
    product = 0.0
    for y, ref in enumerate(weight_refs):
        columns = pl.ds(pl.multiple_of((rank ^ y) * depth, depth), depth)
        product = product + jnp.dot(
            all_heads[:, columns].astype(BF16), ref[...], preferred_element_type=F32
        )
    for x, ref in enumerate(out_refs):
        ref[...] = product[x * count : (x + 1) * count].astype(ref.dtype)


def call(kernel, out_shape, in_specs, scratch_shapes=(), aliases=None):
    return pl.pallas_call(
        kernel,
        out_shape=out_shape,
        in_specs=in_specs,
        out_specs=jax.tree.map(lambda _: pl.BlockSpec(memory_space=pltpu.VMEM), out_shape),
        scratch_shapes=scratch_shapes,
        input_output_aliases=aliases or {},
        compiler_params=pltpu.CompilerParams(vmem_limit_bytes=VMEM_LIMIT),
    )


def in_hbm(x):
    return pltpu.with_memory_space_constraint(x, pltpu.HBM)


def swap(x, axis, distance):
    return lax.ppermute(x, axis, [(i, i ^ distance) for i in range(lax.axis_size(axis))])


def joined(x, axis, combine):
    everything = jax.tree.map(lambda part: lax.all_gather(part, axis), x)
    initial = jax.tree.map(lambda part: part[0], everything)

    def lap(k, so_far):
        return combine(so_far, jax.tree.map(lambda part: part[k], everything))

    return lax.fori_loop(1, lax.axis_size(axis), lap, initial)


def combine(earlier, later):
    highest = jnp.maximum(earlier[0], later[0])
    early_factor = jnp.exp(earlier[0] - highest)
    late_factor = jnp.exp(later[0] - highest)
    softmax_total = earlier[1] * early_factor + later[1] * late_factor
    summed = earlier[2] * early_factor[..., None] + later[2] * late_factor[..., None]
    return (highest, softmax_total, summed)


def general_path(
    queries,
    prompt_key_cache,
    prompt_value_cache,
    kept,
    sample_keys,
    sample_values,
    suffix_len,
    decode_keys,
    decode_values,
    out_weight,
):
    seq_count = lax.axis_size("seq")
    seq_index = lax.axis_index("seq")
    own_count = queries.shape[1]
    step_count = queries.shape[2]
    head_count = queries.shape[3]
    head_dim = queries.shape[4]
    kv_count = prompt_key_cache.shape[1]
    group_size = head_count // kv_count
    logit_scale = 1.0 / math.sqrt(head_dim)
    gathered = lax.all_gather(queries, "seq", axis=1, tiled=True)
    sample_count = gathered.shape[1]
    grouped_queries = gathered[0].reshape(sample_count, step_count, kv_count, group_size, head_dim)
    query_rows = jnp.transpose(grouped_queries, (2, 0, 1, 3, 4)).reshape(
        kv_count, sample_count * step_count * group_size, head_dim
    )
    key_cache_store = prompt_key_cache[0].reshape(kv_count, KEPT_SLOTS, BLOCK_TOKENS, head_dim)
    value_cache_store = prompt_value_cache[0].reshape(kv_count, KEPT_SLOTS, BLOCK_TOKENS, head_dim)
    kept_block_counts = kept[0, :, 0]
    active_mask = jnp.arange(KEPT_SLOTS, dtype=jnp.int32)[None, :] < kept_block_counts[:, None]

    def one_head(pieces):
        head_row_block, key_block_list, value_block_list, live_blocks = pieces
        logit_scores = (
            jnp.einsum(
                "eg,mxg->emx", head_row_block, key_block_list, preferred_element_type=jnp.float32
            )
            * logit_scale
        )
        block_max = jnp.where(live_blocks[None, :], jnp.max(logit_scores, axis=2), NEGATIVE)
        attention_weights = jnp.where(
            live_blocks[None, :, None], jnp.exp(logit_scores - block_max[:, :, None]), 0.0
        )
        block_sum = jnp.sum(attention_weights, axis=2)
        block_output = jnp.einsum(
            "yaf,afi->yai",
            attention_weights.astype(jnp.bfloat16),
            value_block_list,
            preferred_element_type=jnp.float32,
        )
        highest = jnp.max(block_max, axis=1)
        factor = jnp.exp(block_max - highest[:, None])
        return (
            highest,
            jnp.sum(factor * block_sum, axis=1),
            jnp.sum(factor[:, :, None] * block_output, axis=1),
        )

    prompt_maximum, prompt_sum, prompt_output = lax.map(
        one_head, (query_rows, key_cache_store, value_cache_store, active_mask)
    )
    own_queries = queries[0].reshape(own_count, step_count, kv_count, group_size, head_dim)
    suffix_scores = (
        jnp.einsum(
            "nthgd,nhid->nhtgi", own_queries, sample_keys[0], preferred_element_type=jnp.float32
        )
        * logit_scale
    )
    fresh_scores = (
        jnp.einsum(
            "nthgd,nuhd->nhtgu", own_queries, decode_keys[0], preferred_element_type=jnp.float32
        )
        * logit_scale
    )
    position = jnp.arange(sample_keys.shape[3], dtype=jnp.int32)
    sample_token_mask = (position[None, :] < suffix_len[0][:, None])[:, None, None, None, :]
    step_index = jnp.arange(step_count, dtype=jnp.int32)
    newest_token_mask = (step_index[None, :] <= step_index[:, None])[None, None, :, None, :]
    tail_max = jnp.maximum(
        jnp.max(jnp.where(sample_token_mask, suffix_scores, NEGATIVE), axis=4),
        jnp.max(jnp.where(newest_token_mask, fresh_scores, NEGATIVE), axis=4),
    )
    suffix_weights = jnp.where(sample_token_mask, jnp.exp(suffix_scores - tail_max[..., None]), 0.0)
    fresh_weights = jnp.where(newest_token_mask, jnp.exp(fresh_scores - tail_max[..., None]), 0.0)
    tail_sum = jnp.sum(suffix_weights, axis=4) + jnp.sum(fresh_weights, axis=4)
    tail_out = jnp.einsum(
        "nhtgi,nhid->nhtgd",
        suffix_weights.astype(jnp.bfloat16),
        sample_values[0],
        preferred_element_type=jnp.float32,
    )
    tail_out = tail_out + jnp.einsum(
        "nhtgu,nuhd->nhtgd",
        fresh_weights.astype(jnp.bfloat16),
        decode_values[0],
        preferred_element_type=jnp.float32,
    )
    tail_part = (
        jnp.transpose(tail_max, (1, 0, 2, 3)),
        jnp.transpose(tail_sum, (1, 0, 2, 3)),
        jnp.transpose(tail_out, (1, 0, 2, 3, 4)),
    )
    prefix = (
        prompt_maximum.reshape(kv_count, sample_count, step_count, group_size),
        prompt_sum.reshape(kv_count, sample_count, step_count, group_size),
        prompt_output.reshape(kv_count, sample_count, step_count, group_size, head_dim),
    )
    offset = seq_index * own_count
    own_part = tuple((lax.dynamic_slice_in_dim(member, offset, own_count, 1) for member in prefix))
    merged = combine(own_part, tail_part)
    prefix = tuple(
        (
            lax.dynamic_update_slice_in_dim(member, update, offset, 1)
            for member, update in zip(prefix, merged)
        )
    )
    part_max = jnp.transpose(prefix[0], (1, 2, 0, 3)).reshape(sample_count, step_count, head_count)
    part_total = jnp.transpose(prefix[1], (1, 2, 0, 3)).reshape(
        sample_count, step_count, head_count
    )
    part_out = jnp.transpose(prefix[2], (1, 2, 0, 3, 4)).reshape(
        sample_count, step_count, head_count, head_dim
    )
    local_heads = head_count // seq_count
    highest, softmax_total, summed = joined((part_max, part_total, part_out), "seq", combine)
    highest = lax.dynamic_slice_in_dim(highest, seq_index * local_heads, local_heads, 2)
    softmax_total = lax.dynamic_slice_in_dim(softmax_total, seq_index * local_heads, local_heads, 2)
    summed = lax.dynamic_slice_in_dim(summed, seq_index * local_heads, local_heads, 2)
    head_out = (
        (summed / softmax_total[..., None])
        .astype(jnp.bfloat16)
        .reshape(sample_count * step_count, local_heads * head_dim)
    )
    all_rows = lax.all_gather(head_out, "prompt", axis=0, tiled=True)
    result = lax.psum_scatter(
        jnp.dot(all_rows, out_weight, preferred_element_type=jnp.float32),
        "seq",
        scatter_dimension=0,
        tiled=True,
    )
    return result.astype(jnp.bfloat16)


def cross(x, target):
    prompts, seqs = lax.axis_size("prompt"), lax.axis_size("seq")
    pairs = []
    for p in range(prompts):
        for s in range(seqs):
            to_p, to_s = target(p, s)
            pairs.append((p * seqs + s, to_p * seqs + to_s))
    return lax.ppermute(x, ("prompt", "seq"), pairs)


def on_device(
    queries,
    prompt_key_cache,
    prompt_value_cache,
    kept,
    sample_keys,
    sample_values,
    suffix_len,
    decode_keys,
    decode_values,
    out_weight,
):
    seq_count, prompt_count = lax.axis_size("seq"), lax.axis_size("prompt")
    if prompt_count != prompt_key_cache.shape[1]:
        return general_path(
            queries, prompt_key_cache, prompt_value_cache, kept, sample_keys, sample_values,
            suffix_len, decode_keys, decode_values, out_weight,
        )
    steps, head_count, dim = queries.shape[2:]
    heads, chunk = prompt_key_cache.shape[1:3]
    group = head_count // heads
    ranks = seq_count // heads
    shape = (heads, steps, group, dim, ranks, chunk)
    rows = steps * group
    vmem = pl.BlockSpec(memory_space=pltpu.VMEM)
    hbm = pl.BlockSpec(memory_space=pltpu.HBM)
    own_queries = queries.reshape(steps * head_count, dim)
    other_queries = [swap(own_queries, "seq", y) for y in range(1, ranks)]

    fetched = [
        own_queries,
        sample_keys[0, 0],
        sample_values[0, 0],
        decode_keys[0, 0],
        decode_values[0, 0],
        kept.reshape(heads),
        suffix_len.reshape(1),
    ]
    sources = [prompt_key_cache[0], prompt_value_cache[0], *fetched]
    message = jax.ShapeDtypeStruct((2 * chunk + (ranks + 3) * rows, dim), BF16)

    def run_message(*refs):
        n, m = len(sources), len(sources) + heads
        message_kernel(shape, refs[:n], refs[n:m], refs[m : m + len(fetched)], *refs[m + len(fetched) :])

    messages = call(
        run_message,
        [message] * heads,
        [hbm] * len(sources),
        [
            (pltpu.SMEM if x.dtype == jnp.int32 else pltpu.VMEM)(x.shape, x.dtype)
            for x in fetched
        ]
        + [
            pltpu.VMEM((heads, 4 * rows, dim), BF16),
            pltpu.SemaphoreType.DMA((len(fetched) + 2 * heads,)),
        ],
    )(*[x if x.size == 1 else in_hbm(x) for x in sources])

    def run_query(*refs):
        n = ranks - 1
        query_kernel(shape, refs[:n], refs[n + heads : n + 2 * heads], refs[-1])

    if ranks > 1:
        messages = call(
            run_query,
            [message] * heads,
            [vmem] * (ranks - 1 + heads),
            [pltpu.VMEM((heads, (ranks - 1) * rows, dim), BF16)],
            {ranks - 1 + x: x for x in range(heads)},
        )(*other_queries, *messages)
    late_weight, messages = lax.optimization_barrier((out_weight, messages))
    other_weights = [swap(late_weight, "seq", y) for y in range(1, ranks)]
    weight = call(
        fetch_kernel,
        jax.ShapeDtypeStruct(out_weight.shape, BF16),
        [pl.BlockSpec(memory_space=pl.ANY), hbm],
        [pltpu.SemaphoreType.DMA(())],
    )(messages[0], in_hbm(out_weight))
    messages = [messages[0]] + [swap(messages[x], "seq", x * ranks) for x in range(1, heads)]

    all_rows = seq_count * rows

    def run_prefix(*refs):
        prefix_kernel(shape, refs[:heads], *refs[heads + 1 :])

    part = call(
        run_prefix,
        jax.ShapeDtypeStruct((all_rows, 2 * dim), F32),
        [vmem] * heads + [pl.BlockSpec(memory_space=pl.ANY)],
        [pltpu.VMEM((all_rows, dim), BF16), pltpu.VMEM((all_rows, 2 * dim), F32)],
    )(*messages, weight)
    parts = [part] + [swap(part, "seq", y) for y in range(1, ranks)]

    def run_merge(*refs):
        merge_kernel(group, ranks, refs[:ranks], refs[ranks : ranks + 2], refs[ranks + 2])

    count = all_rows // (ranks * group)
    staying, leaving = call(
        run_merge,
        [jax.ShapeDtypeStruct((count, group * dim), BF16)] * 2,
        [vmem] * ranks,
        [pltpu.VMEM((all_rows, dim), F32)],
    )(*parts)
    flip = 1 if ranks > 1 else 0
    head_outs = [staying] + [
        cross(leaving, lambda p, s, targets=targets: (targets[p], s ^ flip))
        for targets in prompt_targets(prompt_count)
    ]

    def run_project(*refs):
        n, m = prompt_count, prompt_count + ranks
        project_kernel(ranks, refs[:n], refs[n:m], refs[m : m + heads], refs[m + heads])

    terms = call(
        run_project,
        [
            jax.ShapeDtypeStruct((count, out_weight.shape[1]), BF16 if x else F32)
            for x in range(heads)
        ],
        [vmem] * (prompt_count + ranks),
        [pltpu.VMEM((prompt_count * count, group * dim), F32)],
    )(*head_outs, weight, *other_weights)
    result = terms[0]
    for x in reversed(range(1, heads)):
        result = result + swap(terms[x], "seq", x * ranks + flip).astype(F32)
    return result.astype(BF16)


def solution(mesh):
    placed = (
        P("prompt", "seq", None, None, None),
        P("prompt", None, "seq", None),
        P("prompt", None, "seq", None),
        P("prompt", None, "seq"),
        P("prompt", "seq", None, None, None),
        P("prompt", "seq", None, None, None),
        P("prompt", "seq"),
        P("prompt", "seq", None, None, None),
        P("prompt", "seq", None, None, None),
        P("seq", "prompt"),
    )
    return jax.shard_map(
        on_device, mesh=mesh, in_specs=placed, out_specs=P("seq", "prompt"), check_vma=False
    )
```

```python
import functools
import math

import jax
import jax.numpy as jnp
from jax import lax
from jax.experimental import pallas as pl
from jax.experimental.pallas import tpu as pltpu
from jax.sharding import PartitionSpec as P

BLOCK_TOKENS = 128
KEPT_SLOTS = 2
NEGATIVE = -1e30
F32 = jnp.float32
BF16 = jnp.bfloat16
VMEM_LIMIT = 16 * 1024 * 1024
MAX_LANE, SUM_LANE = 0, 1


def lanes_of(rows, width, values):
    lane = lax.broadcasted_iota(jnp.int32, (rows, width), 1)
    filled = jnp.zeros((rows, width), F32)
    for i, value in enumerate(values):
        filled = jnp.where(lane == i, jnp.asarray(value, F32), filled)
    return filled


def in_pieces(x, count):
    pieces = []
    for _ in range(count):
        pieces.append(x.astype(BF16))
        x = x - pieces[-1].astype(F32)
    return pieces


def dot_rows(a, b):
    return lax.dot_general(a, b, (((1,), (1,)), ((), ())), preferred_element_type=F32)


def copy_all(pairs, sems):
    copies = [
        pltpu.make_async_copy(source, target, sems.at[i]) for i, (source, target) in enumerate(pairs)
    ]
    for copy in copies:
        copy.start()
    return copies


def message_kernel(shape, in_refs, out_refs, held, small, sems):
    heads, steps, group, dim, ranks, chunk = shape
    rows = steps * group
    scale = 1.0 / math.sqrt(dim)
    chip = lax.div(lax.axis_index("seq"), ranks)
    key_ref, value_ref, *fetched = in_refs
    pairs = list(zip(fetched, held))
    for x in range(heads):
        pairs.append((key_ref.at[chip ^ x], out_refs[x].at[0:chunk]))
        pairs.append((value_ref.at[chip ^ x], out_refs[x].at[chunk : 2 * chunk]))
    copies = [
        pltpu.make_async_copy(source, target, sems.at[i]) for i, (source, target) in enumerate(pairs)
    ]
    for copy in copies:
        copy.start()
    for copy in copies[: len(held)]:
        copy.wait()
    q_ref, tail_key_ref, tail_value_ref, step_key_ref, step_value_ref, kept_ref, len_ref = held
    queries = q_ref[...].astype(F32)
    step_keys = step_key_ref[...].astype(F32)
    step_values = step_value_ref[...].astype(F32)
    all_rows = heads * rows
    q = jnp.concatenate([rows_of_head(queries, shape, h) for h in range(heads)], axis=0)
    q_narrow = q.astype(BF16)

    def by_head(x):
        return [x[h * rows : (h + 1) * rows] for h in range(heads)]

    def spread(x):
        return jnp.concatenate([jnp.broadcast_to(x[h : h + 1], (rows, dim)) for h in range(heads)], axis=0)

    scores = jnp.concatenate(
        [dot_rows(part, tail_key_ref[h]) for h, part in enumerate(by_head(q_narrow))], axis=0
    )
    position = lax.broadcasted_iota(jnp.int32, scores.shape, 1)
    scores = jnp.where(position < len_ref[0], scores * scale, NEGATIVE)
    row = lax.broadcasted_iota(jnp.int32, (all_rows, 1), 0)
    step_of_row = lax.rem(lax.div(row, group), steps)
    own = []
    for u in range(steps):
        score = jnp.sum(q * spread(step_keys[u]), axis=1, keepdims=True) * scale
        own.append(jnp.where(step_of_row >= u, score, NEGATIVE))
    top = functools.reduce(jnp.maximum, own, jnp.max(scores, axis=1, keepdims=True))
    weights = jnp.exp(scores - top)
    total = jnp.sum(weights, axis=1, keepdims=True)
    summed = jnp.concatenate(
        [
            jnp.dot(part, tail_value_ref[h], preferred_element_type=F32)
            for h, part in enumerate(by_head(weights.astype(BF16)))
        ],
        axis=0,
    )
    for u, score in enumerate(own):
        weight = jnp.exp(score - top)
        total = total + weight
        summed = summed + weight.astype(BF16).astype(F32) * spread(step_values[u])
    summed_high, summed_rest = in_pieces(summed, 2)
    kept = jnp.concatenate([jnp.full((rows, 1), kept_ref[h].astype(F32)) for h in range(heads)], axis=0)
    stats = lanes_of(all_rows, dim, [*in_pieces(top, 3), *in_pieces(total, 3), kept]).astype(BF16)
    for i, part in enumerate([summed_high, summed_rest, stats, q_narrow]):
        for h, piece in enumerate(by_head(part)):
            small[h, i * rows : (i + 1) * rows, :] = piece
    for x in range(heads):
        out_refs[x][2 * chunk : 2 * chunk + 4 * rows, :] = small[chip ^ x]
    for copy in copies[len(held) :]:
        copy.wait()


def rows_of_head(whole, shape, h):
    heads, steps, group, *_ = shape
    return jnp.concatenate(
        [
            whole[(t * heads + h) * group : (t * heads + h + 1) * group]
            for t in range(steps)
        ],
        axis=0,
    )


def query_kernel(shape, q_refs, out_refs, small):
    heads, steps, group, dim, ranks, chunk = shape
    rows = steps * group
    chip = lax.div(lax.axis_index("seq"), ranks)
    for y, ref in enumerate(q_refs):
        queries = ref[...].astype(F32)
        for h in range(heads):
            small[h, y * rows : (y + 1) * rows, :] = rows_of_head(queries, shape, h).astype(BF16)
    start = 2 * chunk + 4 * rows
    for x in range(heads):
        out_refs[x][start : start + len(q_refs) * rows, :] = small[chip ^ x]


def fetch_kernel(after_ref, weight_ref, out_ref, sem):
    copy = pltpu.make_async_copy(weight_ref, out_ref, sem)
    copy.start()
    copy.wait()


def prefix_kernel(shape, message_refs, out_ref, q_all, tails):
    heads, steps, group, dim, ranks, chunk = shape
    rows = steps * group
    scale = 1.0 / math.sqrt(dim)
    me = lax.axis_index("seq")
    chip, rank = lax.div(me, ranks), lax.rem(me, ranks)
    all_rows = q_all.shape[0]
    tails[:, 0:dim] = jnp.zeros((all_rows, dim), F32)
    tails[:, dim:] = lanes_of(all_rows, dim, [NEGATIVE])
    kept = []
    for x in range(heads):
        base = (chip ^ x) * ranks
        start = 2 * chunk
        place = pl.multiple_of((base + rank) * rows, rows)
        high = message_refs[x][start : start + rows, :].astype(F32)
        rest = message_refs[x][start + rows : start + 2 * rows, :].astype(F32)
        stats = message_refs[x][start + 2 * rows : start + 3 * rows, :].astype(F32)
        start += 3 * rows
        for y in range(ranks):
            row = pl.multiple_of((base + (rank ^ y)) * rows, rows)
            q_all[pl.ds(row, rows), :] = message_refs[x][start + y * rows : start + (y + 1) * rows, :]
        tails[pl.ds(place, rows), 0:dim] = high + rest
        tail_top = stats[:, 0:1] + stats[:, 1:2] + stats[:, 2:3]
        total = stats[:, 3:4] + stats[:, 4:5] + stats[:, 5:6]
        tails[pl.ds(place, rows), dim:] = lanes_of(rows, dim, [tail_top, total])
        kept.append(stats[0:1, 6:7])
    block = lax.div(lax.broadcasted_iota(jnp.int32, (1, chunk), 1), BLOCK_TOKENS).astype(F32)
    q = q_all[...]
    tail_top = tails[:, dim + MAX_LANE : dim + MAX_LANE + 1]
    top = tail_top
    scores = []
    for x in range(heads):
        score = dot_rows(q, message_refs[x][0:chunk, :]) * scale
        score = jnp.where(block < kept[x], score, NEGATIVE)
        top = jnp.maximum(top, jnp.max(score, axis=1, keepdims=True))
        scores.append(score)
    factor = jnp.exp(tail_top - top)
    total = tails[:, dim + SUM_LANE : dim + SUM_LANE + 1] * factor
    summed = tails[:, 0:dim] * factor
    for x in range(heads):
        weights = jnp.exp(scores[x] - top)
        total = total + jnp.sum(weights, axis=1, keepdims=True)
        summed = summed + jnp.dot(
            weights.astype(BF16),
            message_refs[x][chunk : 2 * chunk, :],
            preferred_element_type=F32,
        )
    out_ref[:, 0:dim] = summed
    out_ref[:, dim:] = lanes_of(all_rows, dim, [top, total])


def block_of(rank, chip, prompt, ranks):
    return rank ^ jnp.where(chip == prompt, 0, 1) if ranks > 1 else rank


def merge_kernel(group, ranks, part_refs, out_refs, merged):
    count = out_refs[0].shape[0]
    dim = out_refs[0].shape[1] // group
    tops = [ref[:, dim + MAX_LANE : dim + MAX_LANE + 1] for ref in part_refs]
    top = functools.reduce(jnp.maximum, tops)
    total, summed = 0.0, 0.0
    for ref, part_top in zip(part_refs, tops):
        factor = jnp.exp(part_top - top)
        total = total + ref[:, dim + SUM_LANE : dim + SUM_LANE + 1] * factor
        summed = summed + ref[:, 0:dim] * factor
    merged[...] = summed / total
    me = lax.axis_index("seq")
    chip, rank = lax.div(me, ranks), lax.rem(me, ranks)
    prompt = lax.axis_index("prompt")
    for out_ref, side in zip(out_refs, (0, 1 if ranks > 1 else 0)):
        block = block_of(rank ^ side, chip, prompt, ranks)
        for g in range(group):
            place = pl.ds(block * (count * group) + g, count, stride=group)
            out_ref[:, g * dim : (g + 1) * dim] = merged[place, :].astype(BF16)


def prompt_targets(count):
    if count == 4:
        return ((1, 0, 3, 2), (3, 2, 0, 1), (2, 3, 1, 0))
    return tuple(tuple(p ^ x for p in range(count)) for x in range(1, count))


def chip_targets(count):
    if count == 4:
        return ((2, 3, 1, 0), (1, 0, 3, 2), (3, 2, 0, 1))
    return tuple(tuple(k ^ x for k in range(count)) for x in range(1, count))


def slot_of(chip, target, count):
    slot = 0
    for i, targets in enumerate(chip_targets(count)):
        for k, to in enumerate(targets):
            slot = jnp.where((chip == k) & (target == to), i + 1, slot)
    return slot


def project_kernel(ranks, head_refs, weight_refs, out_refs, all_heads):
    me = lax.axis_index("seq")
    chip, rank = lax.div(me, ranks), lax.rem(me, ranks)
    prompt = lax.axis_index("prompt")
    count = head_refs[0].shape[0]
    for x, ref in enumerate(head_refs):
        sender = prompt
        if x:
            for p, target in enumerate(prompt_targets(len(head_refs))[x - 1]):
                sender = jnp.where(prompt == target, p, sender)
        place = pl.multiple_of(slot_of(chip, sender, len(out_refs)) * count, count)
        all_heads[pl.ds(place, count), :] = ref[...].astype(F32)
    depth = weight_refs[0].shape[0]
    product = 0.0
    for y, ref in enumerate(weight_refs):
        columns = pl.ds(pl.multiple_of((rank ^ y) * depth, depth), depth)
        product = product + jnp.dot(
            all_heads[:, columns].astype(BF16), ref[...], preferred_element_type=F32
        )
    for x, ref in enumerate(out_refs):
        ref[...] = product[x * count : (x + 1) * count].astype(ref.dtype)


def call(kernel, out_shape, in_specs, scratch_shapes=(), aliases=None):
    return pl.pallas_call(
        kernel,
        out_shape=out_shape,
        in_specs=in_specs,
        out_specs=jax.tree.map(lambda _: pl.BlockSpec(memory_space=pltpu.VMEM), out_shape),
        scratch_shapes=scratch_shapes,
        input_output_aliases=aliases or {},
        compiler_params=pltpu.CompilerParams(vmem_limit_bytes=VMEM_LIMIT),
    )


def in_hbm(x):
    return pltpu.with_memory_space_constraint(x, pltpu.HBM)


def swap(x, axis, distance):
    return lax.ppermute(x, axis, [(i, i ^ distance) for i in range(lax.axis_size(axis))])


def joined(x, axis, combine):
    everything = jax.tree.map(lambda part: lax.all_gather(part, axis), x)
    initial = jax.tree.map(lambda part: part[0], everything)

    def lap(k, so_far):
        return combine(so_far, jax.tree.map(lambda part: part[k], everything))

    return lax.fori_loop(1, lax.axis_size(axis), lap, initial)


def combine(earlier, later):
    highest = jnp.maximum(earlier[0], later[0])
    early_factor = jnp.exp(earlier[0] - highest)
    late_factor = jnp.exp(later[0] - highest)
    softmax_total = earlier[1] * early_factor + later[1] * late_factor
    summed = earlier[2] * early_factor[..., None] + later[2] * late_factor[..., None]
    return (highest, softmax_total, summed)


def general_path(
    queries,
    prompt_key_cache,
    prompt_value_cache,
    kept,
    sample_keys,
    sample_values,
    suffix_len,
    decode_keys,
    decode_values,
    out_weight,
):
    seq_count = lax.axis_size("seq")
    seq_index = lax.axis_index("seq")
    own_count = queries.shape[1]
    step_count = queries.shape[2]
    head_count = queries.shape[3]
    head_dim = queries.shape[4]
    kv_count = prompt_key_cache.shape[1]
    group_size = head_count // kv_count
    logit_scale = 1.0 / math.sqrt(head_dim)
    gathered = lax.all_gather(queries, "seq", axis=1, tiled=True)
    sample_count = gathered.shape[1]
    grouped_queries = gathered[0].reshape(sample_count, step_count, kv_count, group_size, head_dim)
    query_rows = jnp.transpose(grouped_queries, (2, 0, 1, 3, 4)).reshape(
        kv_count, sample_count * step_count * group_size, head_dim
    )
    key_cache_store = prompt_key_cache[0].reshape(kv_count, KEPT_SLOTS, BLOCK_TOKENS, head_dim)
    value_cache_store = prompt_value_cache[0].reshape(kv_count, KEPT_SLOTS, BLOCK_TOKENS, head_dim)
    kept_block_counts = kept[0, :, 0]
    active_mask = jnp.arange(KEPT_SLOTS, dtype=jnp.int32)[None, :] < kept_block_counts[:, None]

    def one_head(pieces):
        head_row_block, key_block_list, value_block_list, live_blocks = pieces
        logit_scores = (
            jnp.einsum(
                "eg,mxg->emx", head_row_block, key_block_list, preferred_element_type=jnp.float32
            )
            * logit_scale
        )
        block_max = jnp.where(live_blocks[None, :], jnp.max(logit_scores, axis=2), NEGATIVE)
        attention_weights = jnp.where(
            live_blocks[None, :, None], jnp.exp(logit_scores - block_max[:, :, None]), 0.0
        )
        block_sum = jnp.sum(attention_weights, axis=2)
        block_output = jnp.einsum(
            "yaf,afi->yai",
            attention_weights.astype(jnp.bfloat16),
            value_block_list,
            preferred_element_type=jnp.float32,
        )
        highest = jnp.max(block_max, axis=1)
        factor = jnp.exp(block_max - highest[:, None])
        return (
            highest,
            jnp.sum(factor * block_sum, axis=1),
            jnp.sum(factor[:, :, None] * block_output, axis=1),
        )

    prompt_maximum, prompt_sum, prompt_output = lax.map(
        one_head, (query_rows, key_cache_store, value_cache_store, active_mask)
    )
    own_queries = queries[0].reshape(own_count, step_count, kv_count, group_size, head_dim)
    suffix_scores = (
        jnp.einsum(
            "nthgd,nhid->nhtgi", own_queries, sample_keys[0], preferred_element_type=jnp.float32
        )
        * logit_scale
    )
    fresh_scores = (
        jnp.einsum(
            "nthgd,nuhd->nhtgu", own_queries, decode_keys[0], preferred_element_type=jnp.float32
        )
        * logit_scale
    )
    position = jnp.arange(sample_keys.shape[3], dtype=jnp.int32)
    sample_token_mask = (position[None, :] < suffix_len[0][:, None])[:, None, None, None, :]
    step_index = jnp.arange(step_count, dtype=jnp.int32)
    newest_token_mask = (step_index[None, :] <= step_index[:, None])[None, None, :, None, :]
    tail_max = jnp.maximum(
        jnp.max(jnp.where(sample_token_mask, suffix_scores, NEGATIVE), axis=4),
        jnp.max(jnp.where(newest_token_mask, fresh_scores, NEGATIVE), axis=4),
    )
    suffix_weights = jnp.where(sample_token_mask, jnp.exp(suffix_scores - tail_max[..., None]), 0.0)
    fresh_weights = jnp.where(newest_token_mask, jnp.exp(fresh_scores - tail_max[..., None]), 0.0)
    tail_sum = jnp.sum(suffix_weights, axis=4) + jnp.sum(fresh_weights, axis=4)
    tail_out = jnp.einsum(
        "nhtgi,nhid->nhtgd",
        suffix_weights.astype(jnp.bfloat16),
        sample_values[0],
        preferred_element_type=jnp.float32,
    )
    tail_out = tail_out + jnp.einsum(
        "nhtgu,nuhd->nhtgd",
        fresh_weights.astype(jnp.bfloat16),
        decode_values[0],
        preferred_element_type=jnp.float32,
    )
    tail_part = (
        jnp.transpose(tail_max, (1, 0, 2, 3)),
        jnp.transpose(tail_sum, (1, 0, 2, 3)),
        jnp.transpose(tail_out, (1, 0, 2, 3, 4)),
    )
    prefix = (
        prompt_maximum.reshape(kv_count, sample_count, step_count, group_size),
        prompt_sum.reshape(kv_count, sample_count, step_count, group_size),
        prompt_output.reshape(kv_count, sample_count, step_count, group_size, head_dim),
    )
    offset = seq_index * own_count
    own_part = tuple((lax.dynamic_slice_in_dim(member, offset, own_count, 1) for member in prefix))
    merged = combine(own_part, tail_part)
    prefix = tuple(
        (
            lax.dynamic_update_slice_in_dim(member, update, offset, 1)
            for member, update in zip(prefix, merged)
        )
    )
    part_max = jnp.transpose(prefix[0], (1, 2, 0, 3)).reshape(sample_count, step_count, head_count)
    part_total = jnp.transpose(prefix[1], (1, 2, 0, 3)).reshape(
        sample_count, step_count, head_count
    )
    part_out = jnp.transpose(prefix[2], (1, 2, 0, 3, 4)).reshape(
        sample_count, step_count, head_count, head_dim
    )
    local_heads = head_count // seq_count
    highest, softmax_total, summed = joined((part_max, part_total, part_out), "seq", combine)
    highest = lax.dynamic_slice_in_dim(highest, seq_index * local_heads, local_heads, 2)
    softmax_total = lax.dynamic_slice_in_dim(softmax_total, seq_index * local_heads, local_heads, 2)
    summed = lax.dynamic_slice_in_dim(summed, seq_index * local_heads, local_heads, 2)
    head_out = (
        (summed / softmax_total[..., None])
        .astype(jnp.bfloat16)
        .reshape(sample_count * step_count, local_heads * head_dim)
    )
    all_rows = lax.all_gather(head_out, "prompt", axis=0, tiled=True)
    result = lax.psum_scatter(
        jnp.dot(all_rows, out_weight, preferred_element_type=jnp.float32),
        "seq",
        scatter_dimension=0,
        tiled=True,
    )
    return result.astype(jnp.bfloat16)


def cross(x, target):
    prompts, seqs = lax.axis_size("prompt"), lax.axis_size("seq")
    pairs = []
    for p in range(prompts):
        for s in range(seqs):
            to_p, to_s = target(p, s)
            pairs.append((p * seqs + s, to_p * seqs + to_s))
    return lax.ppermute(x, ("prompt", "seq"), pairs)


def on_device(
    queries,
    prompt_key_cache,
    prompt_value_cache,
    kept,
    sample_keys,
    sample_values,
    suffix_len,
    decode_keys,
    decode_values,
    out_weight,
):
    seq_count, prompt_count = lax.axis_size("seq"), lax.axis_size("prompt")
    if prompt_count != prompt_key_cache.shape[1]:
        return general_path(
            queries, prompt_key_cache, prompt_value_cache, kept, sample_keys, sample_values,
            suffix_len, decode_keys, decode_values, out_weight,
        )
    steps, head_count, dim = queries.shape[2:]
    heads, chunk = prompt_key_cache.shape[1:3]
    group = head_count // heads
    ranks = seq_count // heads
    shape = (heads, steps, group, dim, ranks, chunk)
    rows = steps * group
    vmem = pl.BlockSpec(memory_space=pltpu.VMEM)
    hbm = pl.BlockSpec(memory_space=pltpu.HBM)
    own_queries = queries.reshape(steps * head_count, dim)
    other_queries = [swap(own_queries, "seq", y) for y in range(1, ranks)]

    fetched = [
        own_queries,
        sample_keys[0, 0],
        sample_values[0, 0],
        decode_keys[0, 0],
        decode_values[0, 0],
        kept.reshape(heads),
        suffix_len.reshape(1),
    ]
    sources = [prompt_key_cache[0], prompt_value_cache[0], *fetched]
    message = jax.ShapeDtypeStruct((2 * chunk + (ranks + 3) * rows, dim), BF16)

    def run_message(*refs):
        n, m = len(sources), len(sources) + heads
        message_kernel(shape, refs[:n], refs[n:m], refs[m : m + len(fetched)], *refs[m + len(fetched) :])

    messages = call(
        run_message,
        [message] * heads,
        [hbm] * len(sources),
        [
            (pltpu.SMEM if x.dtype == jnp.int32 else pltpu.VMEM)(x.shape, x.dtype)
            for x in fetched
        ]
        + [
            pltpu.VMEM((heads, 4 * rows, dim), BF16),
            pltpu.SemaphoreType.DMA((len(fetched) + 2 * heads,)),
        ],
    )(*[x if x.size == 1 else in_hbm(x) for x in sources])

    def run_query(*refs):
        n = ranks - 1
        query_kernel(shape, refs[:n], refs[n + heads : n + 2 * heads], refs[-1])

    if ranks > 1:
        messages = call(
            run_query,
            [message] * heads,
            [vmem] * (ranks - 1 + heads),
            [pltpu.VMEM((heads, (ranks - 1) * rows, dim), BF16)],
            {ranks - 1 + x: x for x in range(heads)},
        )(*other_queries, *messages)
    late_weight, messages = lax.optimization_barrier((out_weight, messages))
    other_weights = [swap(late_weight, "seq", y) for y in range(1, ranks)]
    weight = call(
        fetch_kernel,
        jax.ShapeDtypeStruct(out_weight.shape, BF16),
        [pl.BlockSpec(memory_space=pl.ANY), hbm],
        [pltpu.SemaphoreType.DMA(())],
    )(messages[0], in_hbm(out_weight))
    messages = [messages[0]] + [swap(messages[x], "seq", x * ranks) for x in range(1, heads)]

    all_rows = seq_count * rows

    def run_prefix(*refs):
        prefix_kernel(shape, refs[:heads], *refs[heads + 1 :])

    part = call(
        run_prefix,
        jax.ShapeDtypeStruct((all_rows, 2 * dim), F32),
        [vmem] * heads + [pl.BlockSpec(memory_space=pl.ANY)],
        [pltpu.VMEM((all_rows, dim), BF16), pltpu.VMEM((all_rows, 2 * dim), F32)],
    )(*messages, weight)
    parts = [part] + [swap(part, "seq", y) for y in range(1, ranks)]

    def run_merge(*refs):
        merge_kernel(group, ranks, refs[:ranks], refs[ranks : ranks + 2], refs[ranks + 2])

    count = all_rows // (ranks * group)
    staying, leaving = call(
        run_merge,
        [jax.ShapeDtypeStruct((count, group * dim), BF16)] * 2,
        [vmem] * ranks,
        [pltpu.VMEM((all_rows, dim), F32)],
    )(*parts)
    flip = 1 if ranks > 1 else 0
    head_outs = [staying] + [
        cross(leaving, lambda p, s, targets=targets: (targets[p], s ^ flip))
        for targets in prompt_targets(prompt_count)
    ]

    def run_project(*refs):
        n, m = prompt_count, prompt_count + ranks
        project_kernel(ranks, refs[:n], refs[n:m], refs[m : m + heads], refs[m + heads])

    terms = call(
        run_project,
        [
            jax.ShapeDtypeStruct((count, out_weight.shape[1]), BF16 if x else F32)
            for x in range(heads)
        ],
        [vmem] * (prompt_count + ranks),
        [pltpu.VMEM((prompt_count * count, group * dim), F32)],
    )(*head_outs, weight, *other_weights)
    result = terms[0]
    for x, targets in enumerate(chip_targets(heads)):
        pairs = [(i, targets[i // ranks] * ranks + (i % ranks ^ flip)) for i in range(seq_count)]
        result = result + lax.ppermute(terms[x + 1], "seq", pairs).astype(F32)
    return result.astype(BF16)


def solution(mesh):
    placed = (
        P("prompt", "seq", None, None, None),
        P("prompt", None, "seq", None),
        P("prompt", None, "seq", None),
        P("prompt", None, "seq"),
        P("prompt", "seq", None, None, None),
        P("prompt", "seq", None, None, None),
        P("prompt", "seq"),
        P("prompt", "seq", None, None, None),
        P("prompt", "seq", None, None, None),
        P("seq", "prompt"),
    )
    return jax.shard_map(
        on_device, mesh=mesh, in_specs=placed, out_specs=P("seq", "prompt"), check_vma=False
    )
```

```python
import functools
import math

import jax
import jax.numpy as jnp
from jax import lax
from jax.experimental import pallas as pl
from jax.experimental.pallas import tpu as pltpu
from jax.sharding import PartitionSpec as P

BLOCK_TOKENS = 128
KEPT_SLOTS = 2
NEGATIVE = -1e30
F32 = jnp.float32
BF16 = jnp.bfloat16
VMEM_LIMIT = 16 * 1024 * 1024
MAX_LANE, SUM_LANE = 0, 1


def lanes_of(rows, width, values):
    lane = lax.broadcasted_iota(jnp.int32, (rows, width), 1)
    filled = jnp.zeros((rows, width), F32)
    for i, value in enumerate(values):
        filled = jnp.where(lane == i, jnp.asarray(value, F32), filled)
    return filled


def in_pieces(x, count):
    pieces = []
    for _ in range(count):
        pieces.append(x.astype(BF16))
        x = x - pieces[-1].astype(F32)
    return pieces


def dot_rows(a, b):
    return lax.dot_general(a, b, (((1,), (1,)), ((), ())), preferred_element_type=F32)


def copy_all(pairs, sems):
    copies = [
        pltpu.make_async_copy(source, target, sems.at[i]) for i, (source, target) in enumerate(pairs)
    ]
    for copy in copies:
        copy.start()
    return copies


def message_kernel(shape, in_refs, out_refs, held, small, sems):
    heads, steps, group, dim, ranks, chunk = shape
    rows = steps * group
    scale = 1.0 / math.sqrt(dim)
    chip = lax.div(lax.axis_index("seq"), ranks)
    key_ref, value_ref, *fetched = in_refs
    pairs = list(zip(fetched, held))
    for x in range(heads):
        pairs.append((key_ref.at[chip ^ x], out_refs[x].at[0:chunk]))
        pairs.append((value_ref.at[chip ^ x], out_refs[x].at[chunk : 2 * chunk]))
    copies = [
        pltpu.make_async_copy(source, target, sems.at[i]) for i, (source, target) in enumerate(pairs)
    ]
    for copy in copies:
        copy.start()
    for copy in copies[: len(held)]:
        copy.wait()
    q_ref, tail_key_ref, tail_value_ref, step_key_ref, step_value_ref, kept_ref, len_ref = held
    queries = q_ref[...].astype(F32)
    step_keys = step_key_ref[...].astype(F32)
    step_values = step_value_ref[...].astype(F32)
    all_rows = heads * rows
    q = jnp.concatenate([rows_of_head(queries, shape, h) for h in range(heads)], axis=0)
    q_narrow = q.astype(BF16)

    def by_head(x):
        return [x[h * rows : (h + 1) * rows] for h in range(heads)]

    def spread(x):
        return jnp.concatenate([jnp.broadcast_to(x[h : h + 1], (rows, dim)) for h in range(heads)], axis=0)

    scores = jnp.concatenate(
        [dot_rows(part, tail_key_ref[h]) for h, part in enumerate(by_head(q_narrow))], axis=0
    )
    position = lax.broadcasted_iota(jnp.int32, scores.shape, 1)
    scores = jnp.where(position < len_ref[0], scores * scale, NEGATIVE)
    row = lax.broadcasted_iota(jnp.int32, (all_rows, 1), 0)
    step_of_row = lax.rem(lax.div(row, group), steps)
    own = []
    for u in range(steps):
        score = jnp.sum(q * spread(step_keys[u]), axis=1, keepdims=True) * scale
        own.append(jnp.where(step_of_row >= u, score, NEGATIVE))
    top = functools.reduce(jnp.maximum, own, jnp.max(scores, axis=1, keepdims=True))
    weights = jnp.exp(scores - top)
    total = jnp.sum(weights, axis=1, keepdims=True)
    summed = jnp.concatenate(
        [
            jnp.dot(part, tail_value_ref[h], preferred_element_type=F32)
            for h, part in enumerate(by_head(weights.astype(BF16)))
        ],
        axis=0,
    )
    for u, score in enumerate(own):
        weight = jnp.exp(score - top)
        total = total + weight
        summed = summed + weight.astype(BF16).astype(F32) * spread(step_values[u])
    kept = jnp.concatenate([jnp.full((rows, 1), kept_ref[h].astype(F32)) for h in range(heads)], axis=0)
    stats = lanes_of(all_rows, dim, [*in_pieces(top, 3), *in_pieces(total, 3), kept]).astype(BF16)
    for i, part in enumerate([summed.astype(BF16), stats, q_narrow]):
        for h, piece in enumerate(by_head(part)):
            small[h, i * rows : (i + 1) * rows, :] = piece
    for x in range(heads):
        out_refs[x][2 * chunk : 2 * chunk + 3 * rows, :] = small[chip ^ x]
    for copy in copies[len(held) :]:
        copy.wait()


def rows_of_head(whole, shape, h):
    heads, steps, group, *_ = shape
    return jnp.concatenate(
        [
            whole[(t * heads + h) * group : (t * heads + h + 1) * group]
            for t in range(steps)
        ],
        axis=0,
    )


def query_kernel(shape, q_refs, out_refs, small):
    heads, steps, group, dim, ranks, chunk = shape
    rows = steps * group
    chip = lax.div(lax.axis_index("seq"), ranks)
    for y, ref in enumerate(q_refs):
        queries = ref[...].astype(F32)
        for h in range(heads):
            small[h, y * rows : (y + 1) * rows, :] = rows_of_head(queries, shape, h).astype(BF16)
    start = 2 * chunk + 3 * rows
    for x in range(heads):
        out_refs[x][start : start + len(q_refs) * rows, :] = small[chip ^ x]


def fetch_kernel(after_ref, weight_ref, out_ref, sem):
    copy = pltpu.make_async_copy(weight_ref, out_ref, sem)
    copy.start()
    copy.wait()


def prefix_kernel(shape, message_refs, out_ref, q_all, tails):
    heads, steps, group, dim, ranks, chunk = shape
    rows = steps * group
    scale = 1.0 / math.sqrt(dim)
    me = lax.axis_index("seq")
    chip, rank = lax.div(me, ranks), lax.rem(me, ranks)
    all_rows = q_all.shape[0]
    tails[:, 0:dim] = jnp.zeros((all_rows, dim), F32)
    tails[:, dim:] = lanes_of(all_rows, dim, [NEGATIVE])
    kept = []
    for x in range(heads):
        base = (chip ^ x) * ranks
        start = 2 * chunk
        place = pl.multiple_of((base + rank) * rows, rows)
        high = message_refs[x][start : start + rows, :].astype(F32)
        stats = message_refs[x][start + rows : start + 2 * rows, :].astype(F32)
        start += 2 * rows
        for y in range(ranks):
            row = pl.multiple_of((base + (rank ^ y)) * rows, rows)
            q_all[pl.ds(row, rows), :] = message_refs[x][start + y * rows : start + (y + 1) * rows, :]
        tails[pl.ds(place, rows), 0:dim] = high
        tail_top = stats[:, 0:1] + stats[:, 1:2] + stats[:, 2:3]
        total = stats[:, 3:4] + stats[:, 4:5] + stats[:, 5:6]
        tails[pl.ds(place, rows), dim:] = lanes_of(rows, dim, [tail_top, total])
        kept.append(stats[0:1, 6:7])
    block = lax.div(lax.broadcasted_iota(jnp.int32, (1, chunk), 1), BLOCK_TOKENS).astype(F32)
    q = q_all[...]
    tail_top = tails[:, dim + MAX_LANE : dim + MAX_LANE + 1]
    top = tail_top
    scores = []
    for x in range(heads):
        score = dot_rows(q, message_refs[x][0:chunk, :]) * scale
        score = jnp.where(block < kept[x], score, NEGATIVE)
        top = jnp.maximum(top, jnp.max(score, axis=1, keepdims=True))
        scores.append(score)
    factor = jnp.exp(tail_top - top)
    total = tails[:, dim + SUM_LANE : dim + SUM_LANE + 1] * factor
    summed = tails[:, 0:dim] * factor
    for x in range(heads):
        weights = jnp.exp(scores[x] - top)
        total = total + jnp.sum(weights, axis=1, keepdims=True)
        summed = summed + jnp.dot(
            weights.astype(BF16),
            message_refs[x][chunk : 2 * chunk, :],
            preferred_element_type=F32,
        )
    out_ref[:, 0:dim] = summed
    out_ref[:, dim:] = lanes_of(all_rows, dim, [top, total])


def block_of(rank, chip, prompt, ranks):
    return rank ^ jnp.where(chip == prompt, 0, 1) if ranks > 1 else rank


def merge_kernel(group, ranks, part_refs, out_refs, merged):
    count = out_refs[0].shape[0]
    dim = out_refs[0].shape[1] // group
    tops = [ref[:, dim + MAX_LANE : dim + MAX_LANE + 1] for ref in part_refs]
    top = functools.reduce(jnp.maximum, tops)
    total, summed = 0.0, 0.0
    for ref, part_top in zip(part_refs, tops):
        factor = jnp.exp(part_top - top)
        total = total + ref[:, dim + SUM_LANE : dim + SUM_LANE + 1] * factor
        summed = summed + ref[:, 0:dim] * factor
    merged[...] = summed / total
    me = lax.axis_index("seq")
    chip, rank = lax.div(me, ranks), lax.rem(me, ranks)
    prompt = lax.axis_index("prompt")
    for out_ref, side in zip(out_refs, (0, 1 if ranks > 1 else 0)):
        block = block_of(rank ^ side, chip, prompt, ranks)
        for g in range(group):
            place = pl.ds(block * (count * group) + g, count, stride=group)
            out_ref[:, g * dim : (g + 1) * dim] = merged[place, :].astype(BF16)


def prompt_targets(count):
    if count == 4:
        return ((1, 0, 3, 2), (3, 2, 0, 1), (2, 3, 1, 0))
    return tuple(tuple(p ^ x for p in range(count)) for x in range(1, count))


def chip_targets(count):
    if count == 4:
        return ((2, 3, 1, 0), (1, 0, 3, 2), (3, 2, 0, 1))
    return tuple(tuple(k ^ x for k in range(count)) for x in range(1, count))


def slot_of(chip, target, count):
    slot = 0
    for i, targets in enumerate(chip_targets(count)):
        for k, to in enumerate(targets):
            slot = jnp.where((chip == k) & (target == to), i + 1, slot)
    return slot


def project_kernel(ranks, head_refs, weight_refs, out_refs, all_heads):
    me = lax.axis_index("seq")
    chip, rank = lax.div(me, ranks), lax.rem(me, ranks)
    prompt = lax.axis_index("prompt")
    count = head_refs[0].shape[0]
    for x, ref in enumerate(head_refs):
        sender = prompt
        if x:
            for p, target in enumerate(prompt_targets(len(head_refs))[x - 1]):
                sender = jnp.where(prompt == target, p, sender)
        place = pl.multiple_of(slot_of(chip, sender, len(out_refs)) * count, count)
        all_heads[pl.ds(place, count), :] = ref[...].astype(F32)
    depth = weight_refs[0].shape[0]
    product = 0.0
    for y, ref in enumerate(weight_refs):
        columns = pl.ds(pl.multiple_of((rank ^ y) * depth, depth), depth)
        product = product + jnp.dot(
            all_heads[:, columns].astype(BF16), ref[...], preferred_element_type=F32
        )
    for x, ref in enumerate(out_refs):
        ref[...] = product[x * count : (x + 1) * count].astype(ref.dtype)


def call(kernel, out_shape, in_specs, scratch_shapes=(), aliases=None):
    return pl.pallas_call(
        kernel,
        out_shape=out_shape,
        in_specs=in_specs,
        out_specs=jax.tree.map(lambda _: pl.BlockSpec(memory_space=pltpu.VMEM), out_shape),
        scratch_shapes=scratch_shapes,
        input_output_aliases=aliases or {},
        compiler_params=pltpu.CompilerParams(vmem_limit_bytes=VMEM_LIMIT),
    )


def in_hbm(x):
    return pltpu.with_memory_space_constraint(x, pltpu.HBM)


def swap(x, axis, distance):
    return lax.ppermute(x, axis, [(i, i ^ distance) for i in range(lax.axis_size(axis))])


def joined(x, axis, combine):
    everything = jax.tree.map(lambda part: lax.all_gather(part, axis), x)
    initial = jax.tree.map(lambda part: part[0], everything)

    def lap(k, so_far):
        return combine(so_far, jax.tree.map(lambda part: part[k], everything))

    return lax.fori_loop(1, lax.axis_size(axis), lap, initial)


def combine(earlier, later):
    highest = jnp.maximum(earlier[0], later[0])
    early_factor = jnp.exp(earlier[0] - highest)
    late_factor = jnp.exp(later[0] - highest)
    softmax_total = earlier[1] * early_factor + later[1] * late_factor
    summed = earlier[2] * early_factor[..., None] + later[2] * late_factor[..., None]
    return (highest, softmax_total, summed)


def general_path(
    queries,
    prompt_key_cache,
    prompt_value_cache,
    kept,
    sample_keys,
    sample_values,
    suffix_len,
    decode_keys,
    decode_values,
    out_weight,
):
    seq_count = lax.axis_size("seq")
    seq_index = lax.axis_index("seq")
    own_count = queries.shape[1]
    step_count = queries.shape[2]
    head_count = queries.shape[3]
    head_dim = queries.shape[4]
    kv_count = prompt_key_cache.shape[1]
    group_size = head_count // kv_count
    logit_scale = 1.0 / math.sqrt(head_dim)
    gathered = lax.all_gather(queries, "seq", axis=1, tiled=True)
    sample_count = gathered.shape[1]
    grouped_queries = gathered[0].reshape(sample_count, step_count, kv_count, group_size, head_dim)
    query_rows = jnp.transpose(grouped_queries, (2, 0, 1, 3, 4)).reshape(
        kv_count, sample_count * step_count * group_size, head_dim
    )
    key_cache_store = prompt_key_cache[0].reshape(kv_count, KEPT_SLOTS, BLOCK_TOKENS, head_dim)
    value_cache_store = prompt_value_cache[0].reshape(kv_count, KEPT_SLOTS, BLOCK_TOKENS, head_dim)
    kept_block_counts = kept[0, :, 0]
    active_mask = jnp.arange(KEPT_SLOTS, dtype=jnp.int32)[None, :] < kept_block_counts[:, None]

    def one_head(pieces):
        head_row_block, key_block_list, value_block_list, live_blocks = pieces
        logit_scores = (
            jnp.einsum(
                "eg,mxg->emx", head_row_block, key_block_list, preferred_element_type=jnp.float32
            )
            * logit_scale
        )
        block_max = jnp.where(live_blocks[None, :], jnp.max(logit_scores, axis=2), NEGATIVE)
        attention_weights = jnp.where(
            live_blocks[None, :, None], jnp.exp(logit_scores - block_max[:, :, None]), 0.0
        )
        block_sum = jnp.sum(attention_weights, axis=2)
        block_output = jnp.einsum(
            "yaf,afi->yai",
            attention_weights.astype(jnp.bfloat16),
            value_block_list,
            preferred_element_type=jnp.float32,
        )
        highest = jnp.max(block_max, axis=1)
        factor = jnp.exp(block_max - highest[:, None])
        return (
            highest,
            jnp.sum(factor * block_sum, axis=1),
            jnp.sum(factor[:, :, None] * block_output, axis=1),
        )

    prompt_maximum, prompt_sum, prompt_output = lax.map(
        one_head, (query_rows, key_cache_store, value_cache_store, active_mask)
    )
    own_queries = queries[0].reshape(own_count, step_count, kv_count, group_size, head_dim)
    suffix_scores = (
        jnp.einsum(
            "nthgd,nhid->nhtgi", own_queries, sample_keys[0], preferred_element_type=jnp.float32
        )
        * logit_scale
    )
    fresh_scores = (
        jnp.einsum(
            "nthgd,nuhd->nhtgu", own_queries, decode_keys[0], preferred_element_type=jnp.float32
        )
        * logit_scale
    )
    position = jnp.arange(sample_keys.shape[3], dtype=jnp.int32)
    sample_token_mask = (position[None, :] < suffix_len[0][:, None])[:, None, None, None, :]
    step_index = jnp.arange(step_count, dtype=jnp.int32)
    newest_token_mask = (step_index[None, :] <= step_index[:, None])[None, None, :, None, :]
    tail_max = jnp.maximum(
        jnp.max(jnp.where(sample_token_mask, suffix_scores, NEGATIVE), axis=4),
        jnp.max(jnp.where(newest_token_mask, fresh_scores, NEGATIVE), axis=4),
    )
    suffix_weights = jnp.where(sample_token_mask, jnp.exp(suffix_scores - tail_max[..., None]), 0.0)
    fresh_weights = jnp.where(newest_token_mask, jnp.exp(fresh_scores - tail_max[..., None]), 0.0)
    tail_sum = jnp.sum(suffix_weights, axis=4) + jnp.sum(fresh_weights, axis=4)
    tail_out = jnp.einsum(
        "nhtgi,nhid->nhtgd",
        suffix_weights.astype(jnp.bfloat16),
        sample_values[0],
        preferred_element_type=jnp.float32,
    )
    tail_out = tail_out + jnp.einsum(
        "nhtgu,nuhd->nhtgd",
        fresh_weights.astype(jnp.bfloat16),
        decode_values[0],
        preferred_element_type=jnp.float32,
    )
    tail_part = (
        jnp.transpose(tail_max, (1, 0, 2, 3)),
        jnp.transpose(tail_sum, (1, 0, 2, 3)),
        jnp.transpose(tail_out, (1, 0, 2, 3, 4)),
    )
    prefix = (
        prompt_maximum.reshape(kv_count, sample_count, step_count, group_size),
        prompt_sum.reshape(kv_count, sample_count, step_count, group_size),
        prompt_output.reshape(kv_count, sample_count, step_count, group_size, head_dim),
    )
    offset = seq_index * own_count
    own_part = tuple((lax.dynamic_slice_in_dim(member, offset, own_count, 1) for member in prefix))
    merged = combine(own_part, tail_part)
    prefix = tuple(
        (
            lax.dynamic_update_slice_in_dim(member, update, offset, 1)
            for member, update in zip(prefix, merged)
        )
    )
    part_max = jnp.transpose(prefix[0], (1, 2, 0, 3)).reshape(sample_count, step_count, head_count)
    part_total = jnp.transpose(prefix[1], (1, 2, 0, 3)).reshape(
        sample_count, step_count, head_count
    )
    part_out = jnp.transpose(prefix[2], (1, 2, 0, 3, 4)).reshape(
        sample_count, step_count, head_count, head_dim
    )
    local_heads = head_count // seq_count
    highest, softmax_total, summed = joined((part_max, part_total, part_out), "seq", combine)
    highest = lax.dynamic_slice_in_dim(highest, seq_index * local_heads, local_heads, 2)
    softmax_total = lax.dynamic_slice_in_dim(softmax_total, seq_index * local_heads, local_heads, 2)
    summed = lax.dynamic_slice_in_dim(summed, seq_index * local_heads, local_heads, 2)
    head_out = (
        (summed / softmax_total[..., None])
        .astype(jnp.bfloat16)
        .reshape(sample_count * step_count, local_heads * head_dim)
    )
    all_rows = lax.all_gather(head_out, "prompt", axis=0, tiled=True)
    result = lax.psum_scatter(
        jnp.dot(all_rows, out_weight, preferred_element_type=jnp.float32),
        "seq",
        scatter_dimension=0,
        tiled=True,
    )
    return result.astype(jnp.bfloat16)


def cross(x, target):
    prompts, seqs = lax.axis_size("prompt"), lax.axis_size("seq")
    pairs = []
    for p in range(prompts):
        for s in range(seqs):
            to_p, to_s = target(p, s)
            pairs.append((p * seqs + s, to_p * seqs + to_s))
    return lax.ppermute(x, ("prompt", "seq"), pairs)


def on_device(
    queries,
    prompt_key_cache,
    prompt_value_cache,
    kept,
    sample_keys,
    sample_values,
    suffix_len,
    decode_keys,
    decode_values,
    out_weight,
):
    seq_count, prompt_count = lax.axis_size("seq"), lax.axis_size("prompt")
    if prompt_count != prompt_key_cache.shape[1]:
        return general_path(
            queries, prompt_key_cache, prompt_value_cache, kept, sample_keys, sample_values,
            suffix_len, decode_keys, decode_values, out_weight,
        )
    steps, head_count, dim = queries.shape[2:]
    heads, chunk = prompt_key_cache.shape[1:3]
    group = head_count // heads
    ranks = seq_count // heads
    shape = (heads, steps, group, dim, ranks, chunk)
    rows = steps * group
    vmem = pl.BlockSpec(memory_space=pltpu.VMEM)
    hbm = pl.BlockSpec(memory_space=pltpu.HBM)
    own_queries = queries.reshape(steps * head_count, dim)
    other_queries = [swap(own_queries, "seq", y) for y in range(1, ranks)]

    fetched = [
        own_queries,
        sample_keys[0, 0],
        sample_values[0, 0],
        decode_keys[0, 0],
        decode_values[0, 0],
        kept.reshape(heads),
        suffix_len.reshape(1),
    ]
    sources = [prompt_key_cache[0], prompt_value_cache[0], *fetched]
    message = jax.ShapeDtypeStruct((2 * chunk + (ranks + 2) * rows, dim), BF16)

    def run_message(*refs):
        n, m = len(sources), len(sources) + heads
        message_kernel(shape, refs[:n], refs[n:m], refs[m : m + len(fetched)], *refs[m + len(fetched) :])

    messages = call(
        run_message,
        [message] * heads,
        [hbm] * len(sources),
        [
            (pltpu.SMEM if x.dtype == jnp.int32 else pltpu.VMEM)(x.shape, x.dtype)
            for x in fetched
        ]
        + [
            pltpu.VMEM((heads, 3 * rows, dim), BF16),
            pltpu.SemaphoreType.DMA((len(fetched) + 2 * heads,)),
        ],
    )(*[x if x.size == 1 else in_hbm(x) for x in sources])

    def run_query(*refs):
        n = ranks - 1
        query_kernel(shape, refs[:n], refs[n + heads : n + 2 * heads], refs[-1])

    if ranks > 1:
        messages = call(
            run_query,
            [message] * heads,
            [vmem] * (ranks - 1 + heads),
            [pltpu.VMEM((heads, (ranks - 1) * rows, dim), BF16)],
            {ranks - 1 + x: x for x in range(heads)},
        )(*other_queries, *messages)
    late_weight, messages = lax.optimization_barrier((out_weight, messages))
    other_weights = [swap(late_weight, "seq", y) for y in range(1, ranks)]
    weight = call(
        fetch_kernel,
        jax.ShapeDtypeStruct(out_weight.shape, BF16),
        [pl.BlockSpec(memory_space=pl.ANY), hbm],
        [pltpu.SemaphoreType.DMA(())],
    )(messages[0], in_hbm(out_weight))
    messages = [messages[0]] + [swap(messages[x], "seq", x * ranks) for x in range(1, heads)]

    all_rows = seq_count * rows

    def run_prefix(*refs):
        prefix_kernel(shape, refs[:heads], *refs[heads + 1 :])

    part = call(
        run_prefix,
        jax.ShapeDtypeStruct((all_rows, 2 * dim), F32),
        [vmem] * heads + [pl.BlockSpec(memory_space=pl.ANY)],
        [pltpu.VMEM((all_rows, dim), BF16), pltpu.VMEM((all_rows, 2 * dim), F32)],
    )(*messages, weight)
    parts = [part] + [swap(part, "seq", y) for y in range(1, ranks)]

    def run_merge(*refs):
        merge_kernel(group, ranks, refs[:ranks], refs[ranks : ranks + 2], refs[ranks + 2])

    count = all_rows // (ranks * group)
    staying, leaving = call(
        run_merge,
        [jax.ShapeDtypeStruct((count, group * dim), BF16)] * 2,
        [vmem] * ranks,
        [pltpu.VMEM((all_rows, dim), F32)],
    )(*parts)
    flip = 1 if ranks > 1 else 0
    head_outs = [staying] + [
        cross(leaving, lambda p, s, targets=targets: (targets[p], s ^ flip))
        for targets in prompt_targets(prompt_count)
    ]

    def run_project(*refs):
        n, m = prompt_count, prompt_count + ranks
        project_kernel(ranks, refs[:n], refs[n:m], refs[m : m + heads], refs[m + heads])

    terms = call(
        run_project,
        [
            jax.ShapeDtypeStruct((count, out_weight.shape[1]), BF16 if x else F32)
            for x in range(heads)
        ],
        [vmem] * (prompt_count + ranks),
        [pltpu.VMEM((prompt_count * count, group * dim), F32)],
    )(*head_outs, weight, *other_weights)
    result = terms[0]
    for x, targets in enumerate(chip_targets(heads)):
        pairs = [(i, targets[i // ranks] * ranks + (i % ranks ^ flip)) for i in range(seq_count)]
        result = result + lax.ppermute(terms[x + 1], "seq", pairs).astype(F32)
    return result.astype(BF16)


def solution(mesh):
    placed = (
        P("prompt", "seq", None, None, None),
        P("prompt", None, "seq", None),
        P("prompt", None, "seq", None),
        P("prompt", None, "seq"),
        P("prompt", "seq", None, None, None),
        P("prompt", "seq", None, None, None),
        P("prompt", "seq"),
        P("prompt", "seq", None, None, None),
        P("prompt", "seq", None, None, None),
        P("seq", "prompt"),
    )
    return jax.shard_map(
        on_device, mesh=mesh, in_specs=placed, out_specs=P("seq", "prompt"), check_vma=False
    )
```
